512 devices in a mesh: peer: 64 (over z, x), head: 8 (over y, core).
Axes of the slice: x: 4, y: 4, z: 16, core: 2. Of those that a mesh axis runs over, the one named last changes fastest.
Arguments:
- queries: bfloat16 [16384, 4096], P('peer', 'head'), parts along dimension 1, may hold values from -128 to 128
- keys: bfloat16 [16384, 1024], P('peer', 'head'), parts along dimension 1, may hold values from -24 to 24
- values: bfloat16 [16384, 1024], P('peer', 'head'), parts along dimension 1, may hold values from -6 to 6
- grad_out: bfloat16 [16384, 4096], P('peer', 'head'), parts along dimension 1, may hold values from -6 to 6
- doc_lengths: int32 [32], replicated, may hold values from 1 to 2048, 16384 in all
Outputs:
- attended: bfloat16 [16384, 4096], P('peer', 'head'), parts along dimension 1
- query_grad: float32 [16384, 4096], P('peer', 'head'), parts along dimension 1
- key_grad: float32 [16384, 1024], P('peer', 'head'), parts along dimension 1
- value_grad: float32 [16384, 1024], P('peer', 'head'), parts along dimension 1
The draws below stay inside these ranges and needn't reach their ends.
There are 8 independent parts, one for each index of `head`. The reference program is written for one: setup_inputs(seed, part) draws one part's arguments, and reference() takes and returns one part's arrays. A program takes and returns all parts, laid end to end along the dimension named above; an argument that names none is the same for every part. Nothing has to cross between parts.
Inputs may be any that keep to these rules, and one draw needn't show every extreme that they name: `doc_lengths`: the lengths sum to 16384; the largest is exactly 2048.
All inputs are finite; a program needn't handle non-finite values.
Results may differ from the reference program's by a relative error of at most 0.02.
Values may be sent and summed in bfloat16 or wider, within the bound.
No kernel may reach another device: no remote copies, remote signals or barrier semaphores. Data moves between devices by JAX's collectives and lax.ppermute only.
A program may use at most 64 MiB of HBM per device.

```python
import math
import jax
import jax.numpy as jnp
import numpy as np
from jax import lax

HD = 128
HQ = 4
TOK_DEV = 256
SPAN = 8
TOKENS = 16384
DOCS = 32


def draw_pair(key):
    base_keys = jnp.clip(jax.random.normal(jax.random.fold_in(key, 11), (TOKENS, HD), jnp.float32), -4.0, 4.0)
    base_queries = jnp.clip(jax.random.normal(jax.random.fold_in(key, 12), (TOKENS, HQ * HD), jnp.float32), -4.0, 4.0)
    return (base_keys, base_queries)


def draw_queries(key, part):
    return draw_pair(key)[1].astype(jnp.bfloat16)


def draw_keys(key, part):
    return draw_pair(key)[0].astype(jnp.bfloat16)


def block_levels(rng, dims, cuts, low, top_value):
    def one(position, blocks):
        steps = jax.random.uniform(jax.random.fold_in(jax.random.fold_in(rng, 6), position), (blocks,), jnp.float32, low / len(cuts), top_value / len(cuts))
        return jnp.repeat(jnp.exp(steps), dims[position] // blocks).reshape((-1,) + (1,) * (len(dims) - position - 1))

    gain = one(*cuts[0])
    for cut in cuts[1:]:
        gain = gain * one(*cut)
    return gain


def profile(count, total, limit, lean):
    weights = [(1 << 20) // math.isqrt(grade ** lean) + 1 for grade in range(2, count + 1)]
    spare, given = total - limit - (count - 1), [1] * (count - 1)
    while spare > 0:
        candidates = [i for i in range(count - 1) if given[i] < limit]
        whole, budget = sum([weights[i] for i in candidates]), spare
        for i in candidates:
            more = min(limit - given[i], max(1, budget * weights[i] // whole), spare)
            given[i] = given[i] + more
            spare = spare - more
    return np.array([limit] + given)


def uneven_parts(key, amount, total, most, slope):
    if amount == 2:
        one = jax.random.randint(key, (), max(1, total - most), min(most, total - 1) + 1)
        return jnp.stack([one, total - one])
    tallies = jnp.asarray(profile(amount, total, most, slope), jnp.int32)
    couples = (amount - 1) // 2
    donor, receiver = tallies[1:1 + 2 * couples:2], tallies[2:2 + 2 * couples:2]
    room = jnp.minimum(donor - 1, most - receiver)
    moved = jax.random.randint(jax.random.fold_in(key, 1), (couples,), 0, 1 << 20) % (room + 1)
    tallies = tallies.at[1:1 + 2 * couples:2].set(donor - moved).at[2:2 + 2 * couples:2].set(receiver + moved)
    return tallies[jax.random.permutation(jax.random.fold_in(key, 2), amount)]


def gaussian(stream_key, extent, scale, most, cuts=(), kind=jnp.bfloat16):
    loudness = block_levels(stream_key, extent, cuts, -0.22, 0.18) if cuts else 1.0
    result = jax.random.normal(stream_key, extent, jnp.float32) * scale * loudness
    return jnp.minimum(jnp.maximum(result, -most), most).astype(kind)


def setup_inputs(seed: int = 0, part: int = 0) -> dict:
    splits = jax.random.split(jax.random.key(seed), 6)
    part_splits = jax.random.split(jax.random.fold_in(splits[5], part), 6)
    queries = draw_queries(jax.random.fold_in(jax.random.fold_in(splits[5], part), 71), part)
    keys = draw_keys(jax.random.fold_in(jax.random.fold_in(splits[5], part), 71), part)
    values = gaussian(part_splits[2], (TOKENS, HD), 1.0, 6.0, ((0, 64),))
    grad_out = gaussian(part_splits[3], (TOKENS, HQ * HD), 1.0, 6.0, ((0, 64),))
    doc_lengths = uneven_parts(splits[4], DOCS, TOKENS, SPAN * TOK_DEV, 2).astype(jnp.int32)
    return dict(queries=queries, keys=keys, values=values, grad_out=grad_out, doc_lengths=doc_lengths)


masked_score = -1.0e30


def doc_index(positions, doc_lengths):
    starts = jnp.cumsum(doc_lengths) - doc_lengths
    hits = (starts[None, :] <= positions[:, None]).astype(jnp.int32)
    return (jnp.sum(hits, axis=1) - 1).astype(jnp.int32)


def reference(queries, keys, values, grad_out, doc_lengths):
    block = TOK_DEV
    reach = SPAN * TOK_DEV
    count = TOKENS // block
    window = reach + block
    scale = HD ** -0.5
    positions = jnp.arange(TOKENS, dtype=jnp.int32)
    docs = doc_index(positions, doc_lengths)
    pad_docs = jnp.concatenate([jnp.full((reach,), -1, jnp.int32), docs])
    pad_keys = jnp.concatenate([jnp.zeros((reach, HD), keys.dtype), keys])
    pad_values = jnp.concatenate([jnp.zeros((reach, HD), values.dtype), values])
    query_heads = queries.reshape(TOKENS, HQ, HD)
    grad_heads = grad_out.reshape(TOKENS, HQ, HD)

    def pieces(index):
        start = (index * block).astype(jnp.int32)
        query_block = lax.dynamic_slice_in_dim(query_heads, start, block, 0).astype(jnp.float32)
        grad_block = lax.dynamic_slice_in_dim(grad_heads, start, block, 0).astype(jnp.float32)
        key_block = lax.dynamic_slice_in_dim(pad_keys, start, window, 0).astype(jnp.float32)
        value_block = lax.dynamic_slice_in_dim(pad_values, start, window, 0).astype(jnp.float32)
        query_docs = lax.dynamic_slice_in_dim(docs, start, block, 0)
        key_docs = lax.dynamic_slice_in_dim(pad_docs, start, window, 0)
        query_pos = start + jnp.arange(block, dtype=jnp.int32)
        key_pos = start - reach + jnp.arange(window, dtype=jnp.int32)
        visible = (query_docs[:, None] == key_docs[None, :]) & (key_pos[None, :] <= query_pos[:, None])
        score = jnp.einsum("qhd,kd->hqk", query_block, key_block) * scale
        return start, query_block, grad_block, key_block, value_block, visible, score

    def forward(index):
        start, query_block, grad_block, key_block, value_block, visible, score = pieces(index)
        score = jnp.where(visible[None], score, masked_score)
        peak = jnp.max(score, axis=2)
        weight = jnp.where(visible[None], jnp.exp(score - peak[:, :, None]), 0.0)
        total = jnp.sum(weight, axis=2)
        rounded = lax.optimization_barrier(weight.astype(jnp.bfloat16)).astype(jnp.float32)
        accum = jnp.einsum("hqk,kd->qhd", rounded, value_block)
        output = (accum / total.T[:, :, None]).astype(jnp.bfloat16)
        return output, peak + jnp.log(total)

    outputs, log_totals = lax.map(forward, jnp.arange(count, dtype=jnp.int32))
    attended = outputs.reshape(TOKENS, HQ, HD)
    row_dots = jnp.sum(grad_heads.astype(jnp.float32) * attended.astype(jnp.float32), axis=2)
    row_dots = row_dots.reshape(count, block, HQ)

    def backward(carry, index):
        key_acc, value_acc = carry
        start, query_block, grad_block, key_block, value_block, visible, score = pieces(index)
        log_total = log_totals[index]
        row_dot = row_dots[index].T
        prob = jnp.where(visible[None], jnp.exp(score - log_total[:, :, None]), 0.0)
        dprob = jnp.einsum("qhd,kd->hqk", grad_block, value_block)
        dscore = prob * (dprob - row_dot[:, :, None]) * scale
        dscore = lax.optimization_barrier(dscore.astype(jnp.bfloat16)).astype(jnp.float32)
        prob_round = lax.optimization_barrier(prob.astype(jnp.bfloat16)).astype(jnp.float32)
        query_part = jnp.einsum("hqk,kd->qhd", dscore, key_block)
        key_part = jnp.einsum("hqk,qhd->kd", dscore, query_block)
        value_part = jnp.einsum("hqk,qhd->kd", prob_round, grad_block)
        key_acc = lax.dynamic_update_slice_in_dim(key_acc, lax.dynamic_slice_in_dim(key_acc, start, window, 0) + key_part, start, 0)
        value_acc = lax.dynamic_update_slice_in_dim(value_acc, lax.dynamic_slice_in_dim(value_acc, start, window, 0) + value_part, start, 0)
        return (key_acc, value_acc), query_part.astype(jnp.float32)

    empty = jnp.zeros((TOKENS + reach, HD), jnp.float32)
    (key_acc, value_acc), query_parts = lax.scan(backward, (empty, empty), jnp.arange(count, dtype=jnp.int32))
    return (attended.reshape(TOKENS, HQ * HD), query_parts.reshape(TOKENS, HQ * HD),
            key_acc[reach:].astype(jnp.float32), value_acc[reach:].astype(jnp.float32))
```

```python
import functools
import math

import jax
import jax.numpy as jnp
from jax import lax
from jax.experimental import pallas as pl
from jax.experimental.pallas import tpu as pltpu
from jax.sharding import PartitionSpec as P

T = 256
D = 128
H = 4
ROW = 4
F32 = jnp.float32
BF16 = jnp.bfloat16
NEG = -1e30
SCALE = D**-0.5
TO_EXP2 = SCALE * math.log2(math.e)
LONG = (((1,), (1,)), ((), ()))
PLAIN = (((1,), (0,)), ((), ()))
VM = pl.BlockSpec(memory_space=pltpu.VMEM)
SM = pl.BlockSpec(memory_space=pltpu.SMEM)


def dot(a, b, dims):
    return lax.dot_general(a, b, dims, preferred_element_type=F32)


def head(ref, h):
    return ref[:, h * D : (h + 1) * D]


def doc_starts(lengths_ref, first):
    place = first + lax.broadcasted_iota(jnp.int32, (1, T), 1)
    start = jnp.int32(0)
    own = jnp.zeros((1, T), jnp.int32)
    for i in range(lengths_ref.shape[0]):
        own = jnp.where(place >= start, start, own)
        start = start + lengths_ref[i]
    return own


def scores(q_ref, g_ref, key, value, hidden, index, p_ref, dp_ref, m_ref, t_ref, r_ref):
    for h in range(H):
        s = dot(key, head(q_ref, h), LONG)
        dp = dot(value, head(g_ref, h), LONG)
        s = jnp.where(hidden, NEG, s)
        m = jnp.max(s, axis=0, keepdims=True)
        p = jnp.exp2((s - m) * TO_EXP2)
        p_ref[index, h] = p
        dp_ref[index, h] = dp
        m_ref[index, h : h + 1] = m
        t_ref[index, h : h + 1] = jnp.sum(p, axis=0, keepdims=True)
        r_ref[index, h : h + 1] = jnp.sum(p * dp, axis=0, keepdims=True)


def near_kernel(lengths_ref, q_ref, g_ref, k_ref, v_ref, z1_ref, z2_ref, p_ref, dp_ref, m_ref, t_ref, r_ref):
    first = lax.axis_index("peer") * T
    starts = doc_starts(lengths_ref, first)
    rows = lax.broadcasted_iota(jnp.int32, (T, 1), 0)
    out = (p_ref, dp_ref, m_ref, t_ref, r_ref)
    ahead = rows > lax.broadcasted_iota(jnp.int32, (1, T), 1)
    hidden = ((rows + first) < starts) | ahead
    scores(q_ref, g_ref, k_ref[...], v_ref[...], hidden, 0, *out)
    for i, ref in ((1, z1_ref), (2, z2_ref)):
        hidden = (rows + (first - i * ROW * T)) < starts
        scores(q_ref, g_ref, ref[:, :D], ref[:, D:], hidden, i, *out)


def slot(i, x):
    column = lax.rem(x + 1 + i // 2, ROW)
    kind = lax.rem(i, 2)
    behind = x - column + jnp.where(kind == 1, ROW, jnp.where(column < x, 0, 2 * ROW))
    return column, kind, behind


def far_kernel(
    lengths_ref, q_ref, g_ref, far_ref, m_in, t_in, r_in,
    back_ref, pb_ref, ds_ref, w_ref, rd_ref,
    p_ref, dp_ref, m_ref, t_ref, r_ref,
):
    peer = lax.axis_index("peer")
    x = lax.rem(peer, ROW)
    first = peer * T
    starts = doc_starts(lengths_ref, first)
    rows = lax.broadcasted_iota(jnp.int32, (T, 1), 0)

    @pl.loop(0, 6)
    def _(i):
        column, kind, behind = slot(i, x)
        hidden = (rows + (first - behind * T)) < starts
        key, value = far_ref[column, kind, :, :D], far_ref[column, kind, :, D:]
        scores(q_ref, g_ref, key, value, hidden, i, p_ref, dp_ref, m_ref, t_ref, r_ref)

    peaks = [m_in[b] for b in range(3)] + [m_ref[b] for b in range(6)]
    totals = [t_in[b] for b in range(3)] + [t_ref[b] for b in range(6)]
    dots = [r_in[b] for b in range(3)] + [r_ref[b] for b in range(6)]
    peak = functools.reduce(jnp.maximum, peaks)
    factors = [jnp.exp2((m - peak) * TO_EXP2) for m in peaks]
    over = 1.0 / sum(f * t for f, t in zip(factors, totals))
    rd_ref[...] = sum(f * r for f, r in zip(factors, dots)) * over
    for b in range(9):
        w_ref[b] = factors[b] * over

    @pl.loop(0, 6)
    def _(i):
        column, kind, _ = slot(i, x)
        dk = jnp.zeros((T, D), F32)
        dv = jnp.zeros((T, D), F32)
        for h in range(H):
            pn = p_ref[i, h] * w_ref[3 + i, h : h + 1]
            ds = (pn * (dp_ref[i, h] - rd_ref[h : h + 1])).astype(BF16)
            pb = pn.astype(BF16)
            pb_ref[i, h] = pb
            ds_ref[i, h] = ds
            dk += dot(ds, head(q_ref, h), PLAIN)
            dv += dot(pb, head(g_ref, h), PLAIN)
        back_ref[column, kind, :, :D] = (dk * SCALE).astype(BF16)
        back_ref[column, kind, :, D:] = dv.astype(BF16)

    back_ref[x] = jnp.zeros((2, T, 2 * D), BF16)


def rest_kernel(
    q_ref, g_ref, k_ref, v_ref, z1_ref, z2_ref, far_ref, p_ref, dp_ref, pb_ref, ds_ref, w_ref, rd_ref,
    out_ref, dq_ref, near_ref, o_acc, dq_acc,
):
    x = lax.rem(lax.axis_index("peer"), ROW)
    for b in range(3):
        key = (k_ref[...], z1_ref[:, :D], z2_ref[:, :D])[b]
        value = (v_ref[...], z1_ref[:, D:], z2_ref[:, D:])[b]
        kt, vt = key.T, value.T
        dk = jnp.zeros((T, D), F32)
        dv = jnp.zeros((T, D), F32)
        for h in range(H):
            pn = p_ref[b, h] * w_ref[b, h : h + 1]
            ds = (pn * (dp_ref[b, h] - rd_ref[h : h + 1])).astype(BF16)
            pb = pn.astype(BF16)
            dk += dot(ds, head(q_ref, h), PLAIN)
            dv += dot(pb, head(g_ref, h), PLAIN)
            o, dq = dot(vt, pb, PLAIN), dot(kt, ds, PLAIN)
            o_acc[h] = o if b == 0 else o_acc[h] + o
            dq_acc[h] = dq if b == 0 else dq_acc[h] + dq
        near_ref[b, :, :D] = dk * SCALE
        near_ref[b, :, D:] = dv

    @pl.loop(0, 6)
    def _(i):
        column, kind, _ = slot(i, x)
        kt, vt = far_ref[column, kind, :, :D].T, far_ref[column, kind, :, D:].T
        for h in range(H):
            o_acc[h] += dot(vt, pb_ref[i, h], PLAIN)
            dq_acc[h] += dot(kt, ds_ref[i, h], PLAIN)

    for h in range(H):
        out_ref[:, h * D : (h + 1) * D] = o_acc[h].T.astype(BF16)
        dq_ref[:, h * D : (h + 1) * D] = dq_acc[h].T * SCALE


def gather_kernel(got_ref, near_ref, own_ref, one_ref, two_ref):
    x = lax.rem(lax.axis_index("peer"), ROW)
    own, one, two = near_ref[0], near_ref[1], near_ref[2]
    for s in range(ROW):
        a, b = got_ref[s, 0].astype(F32), got_ref[s, 1].astype(F32)
        own += jnp.where(s > x, a, 0.0)
        two += jnp.where(s < x, a, 0.0)
        one += jnp.where(s != x, b, 0.0)
    own_ref[...] = own
    one_ref[...] = one.astype(BF16)
    two_ref[...] = two.astype(BF16)


def along_z(block, rows, peers):
    far = rows * ROW
    return lax.ppermute(block, "peer", [(i, i + far) for i in range(peers) if 0 <= i + far < peers])


def call(kernel, out, specs, scratch=(), blocks=0, limit=24):
    return pl.pallas_call(
        kernel,
        out_shape=out,
        in_specs=specs,
        out_specs=tuple(VM for _ in out),
        scratch_shapes=list(scratch),
        compiler_params=pltpu.CompilerParams(vmem_limit_bytes=limit << 20),
        cost_estimate=pl.CostEstimate(
            flops=blocks * H * T * T * D * 4, bytes_accessed=4 << 20, transcendentals=blocks * H * T * T
        ),
    )


def body(queries, keys, values, grad_out, doc_lengths):
    peers = lax.axis_size("peer")
    x = lax.rem(lax.axis_index("peer"), ROW)
    groups = [[z * ROW + i for i in range(ROW)] for z in range(peers // ROW)]
    array = jax.ShapeDtypeStruct
    both = jnp.concatenate([keys, values], axis=1)
    z1 = along_z(both, 1, peers)
    z2 = along_z(both, 2, peers)
    sent = jnp.stack([jnp.stack([jnp.where(t > x, both, z2), z1]) for t in range(ROW)])
    far = lax.all_to_all(sent, "peer", 0, 0, axis_index_groups=groups)
    stats = (H, T)
    p, dp, m, t, r = call(
        near_kernel,
        (array((3, H, T, T), F32),) * 2 + (array((3, *stats), F32),) * 3,
        [SM] + [VM] * 6,
        blocks=3,
        limit=16,
    )(doc_lengths, queries, grad_out, keys, values, z1, z2)
    back, pb, ds, w, rd = call(
        far_kernel,
        (
            array((ROW, 2, T, 2 * D), BF16),
            array((6, H, T, T), BF16),
            array((6, H, T, T), BF16),
            array((9, *stats), F32),
            array(stats, F32),
        ),
        [SM] + [VM] * 6,
        [pltpu.VMEM((6, H, T, T), F32)] * 2 + [pltpu.VMEM((6, *stats), F32)] * 3,
        blocks=6,
        limit=32,
    )(doc_lengths, queries, grad_out, far, m, t, r)
    got = lax.all_to_all(back, "peer", 0, 0, axis_index_groups=groups)
    attended, query_grad, near = call(
        rest_kernel,
        (array((T, H * D), BF16), array((T, H * D), F32), array((3, T, 2 * D), F32)),
        [VM] * 13,
        [pltpu.VMEM((H, D, T), F32)] * 2,
        blocks=9,
        limit=32,
    )(queries, grad_out, keys, values, z1, z2, far, p, dp, pb, ds, w, rd)
    own, one, two = call(
        gather_kernel,
        (array((T, 2 * D), F32), array((T, 2 * D), BF16), array((T, 2 * D), BF16)),
        [VM] * 2,
        limit=8,
    )(got, near)
    total = own + along_z(one, -1, peers).astype(F32) + along_z(two, -2, peers).astype(F32)
    return attended, query_grad, total[:, :D], total[:, D:]


def solution(mesh):
    tokens = P("peer", "head")
    return jax.shard_map(
        body,
        mesh=mesh,
        in_specs=(tokens, tokens, tokens, tokens, P()),
        out_specs=(tokens, tokens, tokens, tokens),
        check_vma=False,
    )
```

```python
import functools
import math

import jax
import jax.numpy as jnp
from jax import lax
from jax.experimental import pallas as pl
from jax.experimental.pallas import tpu as pltpu
from jax.sharding import PartitionSpec as P

T = 256
D = 128
H = 4
ROW = 4
F32 = jnp.float32
BF16 = jnp.bfloat16
NEG = -1e30
SCALE = D**-0.5
TO_EXP2 = SCALE * math.log2(math.e)
LONG = (((1,), (1,)), ((), ()))
PLAIN = (((1,), (0,)), ((), ()))
VM = pl.BlockSpec(memory_space=pltpu.VMEM)
SM = pl.BlockSpec(memory_space=pltpu.SMEM)


def dot(a, b, dims):
    return lax.dot_general(a, b, dims, preferred_element_type=F32)


def head(ref, h):
    return ref[:, h * D : (h + 1) * D]


def doc_starts(lengths_ref, first):
    place = first + lax.broadcasted_iota(jnp.int32, (1, T), 1)
    start = jnp.int32(0)
    own = jnp.zeros((1, T), jnp.int32)
    for i in range(lengths_ref.shape[0]):
        own = jnp.where(place >= start, start, own)
        start = start + lengths_ref[i]
    return own


def scores(q_ref, g_ref, key, value, hidden, index, m_ref, t_ref, r_ref, p_ref=None, dp_ref=None):
    for h in range(H):
        s = dot(key, head(q_ref, h), LONG)
        dp = dot(value, head(g_ref, h), LONG)
        s = jnp.where(hidden, NEG, s)
        m = jnp.max(s, axis=0, keepdims=True)
        p = jnp.exp2((s - m) * TO_EXP2)
        if p_ref is not None:
            p_ref[index, h] = p
            dp_ref[index, h] = dp
        m_ref[index, h : h + 1] = m
        t_ref[index, h : h + 1] = jnp.sum(p, axis=0, keepdims=True)
        r_ref[index, h : h + 1] = jnp.sum(p * dp, axis=0, keepdims=True)


def pair_kernel(k_ref, v_ref, out_ref):
    out_ref[0] = k_ref[...]
    out_ref[1] = v_ref[...]


def pack_kernel(own_ref, z1_ref, z2_ref, out_ref, sem):
    x = lax.rem(lax.axis_index("peer"), ROW)

    def fill(t, kind, ref):
        return pltpu.make_async_copy(ref, out_ref.at[t, kind], sem.at[t, kind])

    for t in range(ROW):
        fill(t, 1, z1_ref).start()

        @pl.when(t > x)
        def _(t=t):
            fill(t, 0, own_ref).start()

        @pl.when(t <= x)
        def _(t=t):
            fill(t, 0, z2_ref).start()

    for t in range(ROW):
        for kind in range(2):
            fill(t, kind, z1_ref).wait()


def near_hidden(first, starts, block):
    rows = lax.broadcasted_iota(jnp.int32, (T, 1), 0)
    hidden = (rows + (first - block * ROW * T)) < starts
    if block == 0:
        hidden = hidden | (rows > lax.broadcasted_iota(jnp.int32, (1, T), 1))
    return hidden


def far_hidden(first, starts, behind):
    rows = lax.broadcasted_iota(jnp.int32, (T, 1), 0)
    return (rows + (first - behind * T)) < starts


def near_kernel(lengths_ref, q_ref, g_ref, own_ref, z1_ref, z2_ref, m_ref, t_ref, r_ref):
    first = lax.axis_index("peer") * T
    starts = doc_starts(lengths_ref, first)
    for i, ref in enumerate((own_ref, z1_ref, z2_ref)):
        scores(q_ref, g_ref, ref[0], ref[1], near_hidden(first, starts, i), i, m_ref, t_ref, r_ref)


def slot(i, x):
    column = lax.rem(x + 1 + i // 2, ROW)
    kind = lax.rem(i, 2)
    behind = x - column + jnp.where(kind == 1, ROW, jnp.where(column < x, 0, 2 * ROW))
    return column, kind, behind


def far_kernel(
    lengths_ref, q_ref, g_ref, far_ref, m_in, t_in, r_in,
    back_ref, peak_ref, over_ref, rd_ref,
    p_ref, dp_ref, m_ref, t_ref, r_ref, w_ref,
):
    peer = lax.axis_index("peer")
    x = lax.rem(peer, ROW)
    first = peer * T
    starts = doc_starts(lengths_ref, first)

    @pl.loop(0, 6)
    def _(i):
        column, kind, behind = slot(i, x)
        hidden = far_hidden(first, starts, behind)
        key, value = far_ref[column, kind, 0], far_ref[column, kind, 1]
        scores(q_ref, g_ref, key, value, hidden, i, m_ref, t_ref, r_ref, p_ref, dp_ref)

    peaks = [m_in[b] for b in range(3)] + [m_ref[b] for b in range(6)]
    totals = [t_in[b] for b in range(3)] + [t_ref[b] for b in range(6)]
    dots = [r_in[b] for b in range(3)] + [r_ref[b] for b in range(6)]
    peak = functools.reduce(jnp.maximum, peaks)
    factors = [jnp.exp2((m - peak) * TO_EXP2) for m in peaks]
    over = 1.0 / sum(f * t for f, t in zip(factors, totals))
    peak_ref[...] = peak
    over_ref[...] = over
    rd_ref[...] = sum(f * r for f, r in zip(factors, dots)) * over
    for b in range(6):
        w_ref[b] = factors[3 + b] * over

    @pl.loop(0, 6)
    def _(i):
        column, kind, _ = slot(i, x)
        dk = jnp.zeros((T, D), F32)
        dv = jnp.zeros((T, D), F32)
        for h in range(H):
            pn = p_ref[i, h] * w_ref[i, h : h + 1]
            ds = (pn * (dp_ref[i, h] - rd_ref[h : h + 1])).astype(BF16)
            dk += dot(ds, head(q_ref, h), PLAIN)
            dv += dot(pn.astype(BF16), head(g_ref, h), PLAIN)
        back_ref[column, kind, 0] = (dk * SCALE).astype(BF16)
        back_ref[column, kind, 1] = dv.astype(BF16)

    back_ref[x] = jnp.zeros((2, 2, T, D), BF16)


def rest_kernel(
    lengths_ref, q_ref, g_ref, own_ref, z1_ref, z2_ref, far_ref, peak_ref, over_ref, rd_ref,
    out_ref, dq_ref, near_ref, o_acc, dq_acc,
):
    peer = lax.axis_index("peer")
    x = lax.rem(peer, ROW)
    first = peer * T
    starts = doc_starts(lengths_ref, first)

    def weights(key, value, hidden, h):
        s = dot(key, head(q_ref, h), LONG)
        dp = dot(value, head(g_ref, h), LONG)
        s = jnp.where(hidden, NEG, s)
        pn = jnp.exp2((s - peak_ref[h : h + 1]) * TO_EXP2) * over_ref[h : h + 1]
        ds = pn * (dp - rd_ref[h : h + 1])
        return pn.astype(BF16), ds.astype(BF16)

    for b, ref in enumerate((own_ref, z1_ref, z2_ref)):
        key, value = ref[0], ref[1]
        hidden = near_hidden(first, starts, b)
        kt, vt = key.T, value.T
        dk = jnp.zeros((T, D), F32)
        dv = jnp.zeros((T, D), F32)
        for h in range(H):
            pb, ds = weights(key, value, hidden, h)
            dk += dot(ds, head(q_ref, h), PLAIN)
            dv += dot(pb, head(g_ref, h), PLAIN)
            o, dq = dot(vt, pb, PLAIN), dot(kt, ds, PLAIN)
            o_acc[h] = o if b == 0 else o_acc[h] + o
            dq_acc[h] = dq if b == 0 else dq_acc[h] + dq
        near_ref[b, 0] = dk * SCALE
        near_ref[b, 1] = dv

    @pl.loop(0, 6)
    def _(i):
        column, kind, behind = slot(i, x)
        hidden = far_hidden(first, starts, behind)
        key, value = far_ref[column, kind, 0], far_ref[column, kind, 1]
        kt, vt = key.T, value.T
        for h in range(H):
            pb, ds = weights(key, value, hidden, h)
            o_acc[h] += dot(vt, pb, PLAIN)
            dq_acc[h] += dot(kt, ds, PLAIN)

    for h in range(H):
        out_ref[:, h * D : (h + 1) * D] = o_acc[h].T.astype(BF16)
        dq_ref[:, h * D : (h + 1) * D] = dq_acc[h].T * SCALE


def gather_kernel(got_ref, near_ref, own_ref, one_ref, two_ref):
    x = lax.rem(lax.axis_index("peer"), ROW)
    own, one, two = near_ref[0], near_ref[1], near_ref[2]
    for s in range(ROW):
        a, b = got_ref[s, 0].astype(F32), got_ref[s, 1].astype(F32)
        own += jnp.where(s > x, a, 0.0)
        two += jnp.where(s < x, a, 0.0)
        one += jnp.where(s != x, b, 0.0)
    own_ref[...] = own
    one_ref[...] = one.astype(BF16)
    two_ref[...] = two.astype(BF16)


def final_kernel(own_ref, one_ref, two_ref, dk_ref, dv_ref):
    dk_ref[...] = own_ref[0] + one_ref[0].astype(F32) + two_ref[0].astype(F32)
    dv_ref[...] = own_ref[1] + one_ref[1].astype(F32) + two_ref[1].astype(F32)


def along_z(block, rows, peers):
    far = rows * ROW
    return lax.ppermute(block, "peer", [(i, i + far) for i in range(peers) if 0 <= i + far < peers])


def call(kernel, out, specs, scratch=(), blocks=0, limit=24, space=VM):
    return pl.pallas_call(
        kernel,
        out_shape=out,
        in_specs=specs,
        out_specs=tuple(space for _ in out),
        scratch_shapes=list(scratch),
        compiler_params=pltpu.CompilerParams(vmem_limit_bytes=limit << 20),
        cost_estimate=pl.CostEstimate(
            flops=blocks * H * T * T * D * 4, bytes_accessed=1 << 20, transcendentals=blocks * H * T * T
        ),
    )


def body(queries, keys, values, grad_out, doc_lengths):
    peers = lax.axis_size("peer")
    groups = [[z * ROW + i for i in range(ROW)] for z in range(peers // ROW)]
    array = jax.ShapeDtypeStruct
    block, sums, stats = (2, T, D), array((2, T, D), F32), (H, T)
    (own,) = call(pair_kernel, (array(block, BF16),), [VM] * 2, limit=4)(keys, values)
    z1 = along_z(own, 1, peers)
    z2 = along_z(own, 2, peers)
    (sent,) = call(
        pack_kernel,
        (array((ROW, 2, *block), BF16),),
        [VM] * 3,
        [pltpu.SemaphoreType.DMA((ROW, 2))],
        limit=4,
        space=pl.BlockSpec(memory_space=pl.ANY),
    )(own, z1, z2)
    far = lax.all_to_all(sent, "peer", 0, 0, axis_index_groups=groups)
    m, t, r = call(near_kernel, (array((3, *stats), F32),) * 3, [SM] + [VM] * 5, blocks=3, limit=8)(
        doc_lengths, queries, grad_out, own, z1, z2
    )
    back, peak, over, rd = call(
        far_kernel,
        (array((ROW, 2, *block), BF16),) + (array(stats, F32),) * 3,
        [SM] + [VM] * 6,
        [pltpu.VMEM((6, H, T, T), F32)] * 2 + [pltpu.VMEM((6, *stats), F32)] * 4,
        blocks=6,
        limit=24,
    )(doc_lengths, queries, grad_out, far, m, t, r)
    got = lax.all_to_all(back, "peer", 0, 0, axis_index_groups=groups)
    attended, query_grad, near = call(
        rest_kernel,
        (array((T, H * D), BF16), array((T, H * D), F32), array((3, *block), F32)),
        [SM] + [VM] * 9,
        [pltpu.VMEM((H, D, T), F32)] * 2,
        blocks=9,
        limit=16,
    )(doc_lengths, queries, grad_out, own, z1, z2, far, peak, over, rd)
    mine, one, two = call(
        gather_kernel, (sums, array(block, BF16), array(block, BF16)), [VM] * 2, limit=8
    )(got, near)
    key_grad, value_grad = call(final_kernel, (array((T, D), F32),) * 2, [VM] * 3, limit=4)(
        mine, along_z(one, -1, peers), along_z(two, -2, peers)
    )
    return attended, query_grad, key_grad, value_grad


def solution(mesh):
    tokens = P("peer", "head")
    return jax.shard_map(
        body,
        mesh=mesh,
        in_specs=(tokens, tokens, tokens, tokens, P()),
        out_specs=(tokens, tokens, tokens, tokens),
        check_vma=False,
    )
```

```python
import functools
import math

import jax
import jax.numpy as jnp
from jax import lax
from jax.experimental import pallas as pl
from jax.experimental.pallas import tpu as pltpu
from jax.sharding import PartitionSpec as P

T = 256
D = 128
H = 4
ROW = 4
F32 = jnp.float32
BF16 = jnp.bfloat16
NEG = -1e30
SCALE = D**-0.5
TO_EXP2 = SCALE * math.log2(math.e)
LONG = (((1,), (1,)), ((), ()))
PLAIN = (((1,), (0,)), ((), ()))
VM = pl.BlockSpec(memory_space=pltpu.VMEM)
ANY = pl.BlockSpec(memory_space=pl.ANY)
SM = pl.BlockSpec(memory_space=pltpu.SMEM)


def dot(a, b, dims):
    return lax.dot_general(a, b, dims, preferred_element_type=F32)


def head(ref, h):
    return ref[:, h * D : (h + 1) * D]


def doc_starts(lengths_ref, first):
    place = first + lax.broadcasted_iota(jnp.int32, (1, T), 1)
    start = jnp.int32(0)
    own = jnp.zeros((1, T), jnp.int32)
    for i in range(lengths_ref.shape[0]):
        own = jnp.where(place >= start, start, own)
        start = start + lengths_ref[i]
    return own


def scores(q_ref, g_ref, key, value, hidden, index, m_ref, t_ref, r_ref, p_ref=None, dp_ref=None):
    for h in range(H):
        s = dot(key, head(q_ref, h), LONG)
        dp = dot(value, head(g_ref, h), LONG)
        s = jnp.where(hidden, NEG, s)
        m = jnp.max(s, axis=0, keepdims=True)
        p = jnp.exp2((s - m) * TO_EXP2)
        if p_ref is not None:
            p_ref[index, h] = p
            dp_ref[index, h] = dp
        m_ref[index, h : h + 1] = m
        t_ref[index, h : h + 1] = jnp.sum(p, axis=0, keepdims=True)
        r_ref[index, h : h + 1] = jnp.sum(p * dp, axis=0, keepdims=True)


def pair_kernel(k_ref, v_ref, out_ref, sem):
    copies = [pltpu.make_async_copy(r, out_ref.at[i], sem.at[i]) for i, r in enumerate((k_ref, v_ref))]
    for copy in copies:
        copy.start()
    for copy in copies:
        copy.wait()


def filler(out_ref, sem):
    x = lax.rem(lax.axis_index("peer"), ROW)

    def fill(i, kind, ref):
        return pltpu.make_async_copy(ref, out_ref.at[lax.rem(x + i, ROW), kind], sem.at[i - 1, kind])

    return x, fill


def pack_own_kernel(own_ref, out_ref, sem):
    x, fill = filler(out_ref, sem)
    for act in ("start", "wait"):
        for i in range(1, ROW):

            @pl.when(x + i < ROW)
            def _(i=i, act=act):
                getattr(fill(i, 0, own_ref), act)()


def pack_rows_kernel(z1_ref, z2_ref, _, out_ref, sem):
    x, fill = filler(out_ref, sem)
    for act in ("start", "wait"):
        for i in range(1, ROW):
            getattr(fill(i, 1, z1_ref), act)()

            @pl.when(x + i >= ROW)
            def _(i=i, act=act):
                getattr(fill(i, 0, z2_ref), act)()


def near_hidden(first, starts, block):
    rows = lax.broadcasted_iota(jnp.int32, (T, 1), 0)
    hidden = (rows + (first - block * ROW * T)) < starts
    if block == 0:
        hidden = hidden | (rows > lax.broadcasted_iota(jnp.int32, (1, T), 1))
    return hidden


def far_hidden(first, starts, behind):
    rows = lax.broadcasted_iota(jnp.int32, (T, 1), 0)
    return (rows + (first - behind * T)) < starts


def near_kernel(lengths_ref, q_ref, g_ref, own_ref, z1_ref, z2_ref, m_ref, t_ref, r_ref):
    first = lax.axis_index("peer") * T
    starts = doc_starts(lengths_ref, first)
    for i, ref in enumerate((own_ref, z1_ref, z2_ref)):
        scores(q_ref, g_ref, ref[0], ref[1], near_hidden(first, starts, i), i, m_ref, t_ref, r_ref)


def slot(i, x):
    column = lax.rem(x + 1 + i // 2, ROW)
    kind = i % 2
    behind = x - column + (ROW if kind else jnp.where(column < x, 0, 2 * ROW))
    return column, kind, behind


def key_side(q_ref, g_ref, pb_ref, ds_ref):
    dk = sum(dot(ds_ref[h], head(q_ref, h), PLAIN) for h in range(H))
    dv = sum(dot(pb_ref[h], head(g_ref, h), PLAIN) for h in range(H))
    return dk * SCALE, dv


def far_kernel(
    lengths_ref, q_ref, g_ref, far_ref, m_in, t_in, r_in,
    back_ref, peak_ref, over_ref, rd_ref,
    p_ref, dp_ref, m_ref, t_ref, r_ref, w_ref, pb_ref, ds_ref, ready_ref, sem,
):
    peer = lax.axis_index("peer")
    x = lax.rem(peer, ROW)
    first = peer * T
    starts = doc_starts(lengths_ref, first)
    for i in range(6):
        column, kind, behind = slot(i, x)
        hidden = far_hidden(first, starts, behind)
        key, value = far_ref[column, kind, 0], far_ref[column, kind, 1]
        scores(q_ref, g_ref, key, value, hidden, i, m_ref, t_ref, r_ref, p_ref, dp_ref)

    peaks = [m_in[b] for b in range(3)] + [m_ref[b] for b in range(6)]
    totals = [t_in[b] for b in range(3)] + [t_ref[b] for b in range(6)]
    dots = [r_in[b] for b in range(3)] + [r_ref[b] for b in range(6)]
    peak = functools.reduce(jnp.maximum, peaks)
    factors = [jnp.exp2((m - peak) * TO_EXP2) for m in peaks]
    over = 1.0 / sum(f * t for f, t in zip(factors, totals))
    peak_ref[...] = peak
    over_ref[...] = over
    rd_ref[...] = sum(f * r for f, r in zip(factors, dots)) * over
    for b in range(6):
        w_ref[b] = factors[3 + b] * over

    copies = []
    for i in range(6):
        column, kind, _ = slot(i, x)
        for h in range(H):
            pn = p_ref[i, h] * w_ref[i, h : h + 1]
            pb_ref[i % 2, h] = pn.astype(BF16)
            ds_ref[i % 2, h] = (pn * (dp_ref[i, h] - rd_ref[h : h + 1])).astype(BF16)
        dk, dv = key_side(q_ref, g_ref, pb_ref.at[i % 2], ds_ref.at[i % 2])
        ready_ref[i, 0] = dk.astype(BF16)
        ready_ref[i, 1] = dv.astype(BF16)
        copies.append(pltpu.make_async_copy(ready_ref.at[i], back_ref.at[column, kind], sem.at[i]))
        copies[-1].start()
    for copy in copies:
        copy.wait()


def rest_kernel(
    lengths_ref, q_ref, g_ref, own_ref, z1_ref, z2_ref, far_ref, peak_ref, over_ref, rd_ref,
    out_ref, dq_ref, near_ref, o_acc, dq_acc, pb_ref, ds_ref,
):
    peer = lax.axis_index("peer")
    x = lax.rem(peer, ROW)
    first = peer * T
    starts = doc_starts(lengths_ref, first)
    near = (own_ref, z1_ref, z2_ref)
    for b in range(9):
        if b < 3:
            key, value = near[b][0], near[b][1]
            hidden = near_hidden(first, starts, b)
        else:
            column, kind, behind = slot(b - 3, x)
            key, value = far_ref[column, kind, 0], far_ref[column, kind, 1]
            hidden = far_hidden(first, starts, behind)
        pb, ds = pb_ref.at[b % 2], ds_ref.at[b % 2]
        for h in range(H):
            s = dot(key, head(q_ref, h), LONG)
            dp = dot(value, head(g_ref, h), LONG)
            s = jnp.where(hidden, NEG, s)
            pn = jnp.exp2((s - peak_ref[h : h + 1]) * TO_EXP2) * over_ref[h : h + 1]
            pb[h] = pn.astype(BF16)
            ds[h] = (pn * (dp - rd_ref[h : h + 1])).astype(BF16)
        kt, vt = key.T, value.T
        for h in range(H):
            o, dq = dot(vt, pb[h], PLAIN), dot(kt, ds[h], PLAIN)
            o_acc[h] = o if b == 0 else o_acc[h] + o
            dq_acc[h] = dq if b == 0 else dq_acc[h] + dq
        if b < 3:
            near_ref[b, 0], near_ref[b, 1] = key_side(q_ref, g_ref, pb, ds)

    for h in range(H):
        out_ref[:, h * D : (h + 1) * D] = o_acc[h].T.astype(BF16)
        dq_ref[:, h * D : (h + 1) * D] = dq_acc[h].T * SCALE


def gather_kernel(got_ref, near_ref, own_ref, one_ref, two_ref):
    x = lax.rem(lax.axis_index("peer"), ROW)
    own, one, two = near_ref[0], near_ref[1], near_ref[2]
    for s in range(ROW):
        a, b = got_ref[s, 0].astype(F32), got_ref[s, 1].astype(F32)
        own += jnp.where(s > x, a, 0.0)
        two += jnp.where(s < x, a, 0.0)
        one += jnp.where(s != x, b, 0.0)
    own_ref[...] = own
    one_ref[...] = one.astype(BF16)
    two_ref[...] = two.astype(BF16)


def final_kernel(own_ref, one_ref, two_ref, dk_ref, dv_ref):
    dk_ref[...] = own_ref[0] + one_ref[0].astype(F32) + two_ref[0].astype(F32)
    dv_ref[...] = own_ref[1] + one_ref[1].astype(F32) + two_ref[1].astype(F32)


def along_z(block, rows, peers):
    far = rows * ROW
    return lax.ppermute(block, "peer", [(i, i + far) for i in range(peers) if 0 <= i + far < peers])


def call(kernel, out, specs, scratch=(), blocks=0, limit=24, first=VM, alias={}):
    return pl.pallas_call(
        kernel,
        out_shape=out,
        in_specs=specs,
        out_specs=(first,) + tuple(VM for _ in out[1:]),
        scratch_shapes=list(scratch),
        input_output_aliases=alias,
        compiler_params=pltpu.CompilerParams(vmem_limit_bytes=limit << 20),
        cost_estimate=pl.CostEstimate(
            flops=blocks * H * T * T * D * 4, bytes_accessed=1 << 20, transcendentals=blocks * H * T * T
        ),
    )


def body(queries, keys, values, grad_out, doc_lengths):
    peers = lax.axis_size("peer")
    groups = [[z * ROW + i for i in range(ROW)] for z in range(peers // ROW)]
    array = jax.ShapeDtypeStruct
    block, sums, stats = (2, T, D), array((2, T, D), F32), (H, T)
    (own,) = call(pair_kernel, (array(block, BF16),), [ANY] * 2, [pltpu.SemaphoreType.DMA((2,))], limit=60)(
        keys, values
    )
    z1 = along_z(own, 1, peers)
    z2 = along_z(own, 2, peers)
    slots = [pltpu.SemaphoreType.DMA((ROW - 1, 2))]
    packed = (array((ROW, 2, *block), BF16),)
    (sent,) = call(pack_own_kernel, packed, [ANY], slots, limit=4, first=ANY)(own)
    (sent,) = call(pack_rows_kernel, packed, [VM, VM, ANY], slots, limit=4, first=ANY, alias={2: 0})(z1, z2, sent)
    far = lax.all_to_all(sent, "peer", 0, 0, axis_index_groups=groups)
    m, t, r = call(near_kernel, (array((3, *stats), F32),) * 3, [SM] + [VM] * 5, blocks=3, limit=8)(
        doc_lengths, queries, grad_out, own, z1, z2
    )
    back, peak, over, rd = call(
        far_kernel,
        (array((ROW, 2, *block), BF16),) + (array(stats, F32),) * 3,
        [SM] + [VM] * 6,
        [pltpu.VMEM((6, H, T, T), F32)] * 2
        + [pltpu.VMEM((6, *stats), F32)] * 4
        + [pltpu.VMEM((2, H, T, T), BF16)] * 2
        + [pltpu.VMEM((6, *block), BF16), pltpu.SemaphoreType.DMA((6,))],
        blocks=6,
        limit=24,
        first=ANY,
    )(doc_lengths, queries, grad_out, far, m, t, r)
    got = lax.all_to_all(back, "peer", 0, 0, axis_index_groups=groups)
    attended, query_grad, near = call(
        rest_kernel,
        (array((T, H * D), BF16), array((T, H * D), F32), array((3, *block), F32)),
        [SM] + [VM] * 9,
        [pltpu.VMEM((H, D, T), F32)] * 2 + [pltpu.VMEM((2, H, T, T), BF16)] * 2,
        blocks=9,
        limit=16,
    )(doc_lengths, queries, grad_out, own, z1, z2, far, peak, over, rd)
    mine, one, two = call(
        gather_kernel, (sums, array(block, BF16), array(block, BF16)), [VM] * 2, limit=8
    )(got, near)
    key_grad, value_grad = call(final_kernel, (array((T, D), F32),) * 2, [VM] * 3, limit=4)(
        mine, along_z(one, -1, peers), along_z(two, -2, peers)
    )
    return attended, query_grad, key_grad, value_grad


def solution(mesh):
    tokens = P("peer", "head")
    return jax.shard_map(
        body,
        mesh=mesh,
        in_specs=(tokens, tokens, tokens, tokens, P()),
        out_specs=(tokens, tokens, tokens, tokens),
        check_vma=False,
    )
```

```python
import functools
import math

import jax
import jax.numpy as jnp
from jax import lax
from jax.experimental import pallas as pl
from jax.experimental.pallas import tpu as pltpu
from jax.sharding import PartitionSpec as P

T = 256
D = 128
H = 4
ROW = 4
F32 = jnp.float32
BF16 = jnp.bfloat16
NEG = -1e30
SCALE = D**-0.5
TO_EXP2 = SCALE * math.log2(math.e)
LONG = (((1,), (1,)), ((), ()))
PLAIN = (((1,), (0,)), ((), ()))
VM = pl.BlockSpec(memory_space=pltpu.VMEM)
ANY = pl.BlockSpec(memory_space=pl.ANY)
SM = pl.BlockSpec(memory_space=pltpu.SMEM)


def dot(a, b, dims):
    return lax.dot_general(a, b, dims, preferred_element_type=F32)


def head(ref, h):
    return ref[:, h * D : (h + 1) * D]


def doc_starts(lengths_ref, first):
    place = first + lax.broadcasted_iota(jnp.int32, (1, T), 1)
    start = jnp.int32(0)
    own = jnp.zeros((1, T), jnp.int32)
    for i in range(lengths_ref.shape[0]):
        own = jnp.where(place >= start, start, own)
        start = start + lengths_ref[i]
    return own


def scores(q_ref, g_ref, key, value, hidden, index, m_ref, t_ref, r_ref, p_ref=None, dp_ref=None):
    for h in range(H):
        s = dot(key, head(q_ref, h), LONG)
        dp = dot(value, head(g_ref, h), LONG)
        s = jnp.where(hidden, NEG, s)
        m = jnp.max(s, axis=0, keepdims=True)
        p = jnp.exp2((s - m) * TO_EXP2)
        if p_ref is not None:
            p_ref[index, h] = p
            dp_ref[index, h] = dp
        m_ref[index, h : h + 1] = m
        t_ref[index, h : h + 1] = jnp.sum(p, axis=0, keepdims=True)
        r_ref[index, h : h + 1] = jnp.sum(p * dp, axis=0, keepdims=True)


def pair_kernel(k_ref, v_ref, out_ref, sem):
    copies = [pltpu.make_async_copy(r, out_ref.at[i], sem.at[i]) for i, r in enumerate((k_ref, v_ref))]
    for copy in copies:
        copy.start()
    for copy in copies:
        copy.wait()


def pack_kernel(own_ref, z1_ref, z2_ref, *out_refs):
    x = lax.rem(lax.axis_index("peer"), ROW)
    for d, ref in enumerate(out_refs, 1):

        @pl.when(x + d < ROW)
        def _(ref=ref):
            ref[0] = own_ref[...]

        @pl.when(x + d >= ROW)
        def _(ref=ref):
            ref[0] = z2_ref[...]

        ref[1] = z1_ref[...]


def near_hidden(first, starts, block):
    rows = lax.broadcasted_iota(jnp.int32, (T, 1), 0)
    hidden = (rows + (first - block * ROW * T)) < starts
    if block == 0:
        hidden = hidden | (rows > lax.broadcasted_iota(jnp.int32, (1, T), 1))
    return hidden


def far_hidden(first, starts, behind):
    rows = lax.broadcasted_iota(jnp.int32, (T, 1), 0)
    return (rows + (first - behind * T)) < starts


def hold_kernel(own_ref, held_ref):
    held_ref[...] = own_ref[...]


def near_kernel(lengths_ref, q_ref, g_ref, own_ref, z1_ref, z2_ref, m_ref, t_ref, r_ref):
    first = lax.axis_index("peer") * T
    starts = doc_starts(lengths_ref, first)
    for i, ref in enumerate((own_ref, z1_ref, z2_ref)):
        scores(q_ref, g_ref, ref[0], ref[1], near_hidden(first, starts, i), i, m_ref, t_ref, r_ref)


def behind(d, kind, x):
    return jnp.where((x >= d) ^ (kind == 1), d, ROW + d)


def key_side(q_ref, g_ref, pb_ref, ds_ref):
    dk = sum(dot(ds_ref[h], head(q_ref, h), PLAIN) for h in range(H))
    dv = sum(dot(pb_ref[h], head(g_ref, h), PLAIN) for h in range(H))
    return dk * SCALE, dv


def far_scores(d, lengths_ref, q_ref, g_ref, far_ref, p_ref, dp_ref, m_ref, t_ref, r_ref):
    peer = lax.axis_index("peer")
    first = peer * T
    starts = doc_starts(lengths_ref, first)
    for i in range(2):
        hidden = far_hidden(first, starts, behind(d, i, lax.rem(peer, ROW)))
        scores(q_ref, g_ref, far_ref[i, 0], far_ref[i, 1], hidden, i, m_ref, t_ref, r_ref, p_ref, dp_ref)


def far_back(p_ref, dp_ref, w_ref, rd_ref, q_ref, g_ref, back_ref, pb_ref, ds_ref):
    for i in range(2):
        for h in range(H):
            pn = p_ref[i, h] * w_ref[i, h : h + 1]
            pb_ref[i, h] = pn.astype(BF16)
            ds_ref[i, h] = (pn * (dp_ref[i, h] - rd_ref[h : h + 1])).astype(BF16)
        dk, dv = key_side(q_ref, g_ref, pb_ref.at[i], ds_ref.at[i])
        back_ref[i, 0] = dk.astype(BF16)
        back_ref[i, 1] = dv.astype(BF16)


def last_kernel(
    d, lengths_ref, q_ref, g_ref, far_ref, mn, tn, rn, m1, t1, r1, m3, t3, r3,
    back_ref, peak_ref, over_ref, rd_ref, w1_ref, w3_ref,
    p_ref, dp_ref, m_ref, t_ref, r_ref, w_ref, pb_ref, ds_ref,
):
    far_scores(d, lengths_ref, q_ref, g_ref, far_ref, p_ref, dp_ref, m_ref, t_ref, r_ref)

    def each(near, *pairs):
        return [near[b] for b in range(3)] + [ref[b] for ref in pairs for b in range(2)]

    peaks, totals, dots = each(mn, m1, m3, m_ref), each(tn, t1, t3, t_ref), each(rn, r1, r3, r_ref)
    peak = functools.reduce(jnp.maximum, peaks)
    factors = [jnp.exp2((m - peak) * TO_EXP2) for m in peaks]
    over = 1.0 / sum(f * t for f, t in zip(factors, totals))
    peak_ref[...] = peak
    over_ref[...] = over
    rd_ref[...] = sum(f * r for f, r in zip(factors, dots)) * over
    for n, ref in enumerate((w1_ref, w3_ref, w_ref)):
        for b in range(2):
            ref[b] = factors[3 + 2 * n + b] * over
    far_back(p_ref, dp_ref, w_ref, rd_ref, q_ref, g_ref, back_ref, pb_ref, ds_ref)


def rest_kernel(
    lengths_ref, q_ref, g_ref, own_ref, z1_ref, z2_ref, f1_ref, f2_ref, f3_ref, peak_ref, over_ref, rd_ref,
    out_ref, dq_ref, near_ref, o_acc, dq_acc, pb_ref, ds_ref,
):
    peer = lax.axis_index("peer")
    x = lax.rem(peer, ROW)
    first = peer * T
    starts = doc_starts(lengths_ref, first)
    near = (own_ref, z1_ref, z2_ref)
    for b in range(9):
        if b < 3:
            key, value = near[b][0], near[b][1]
            hidden = near_hidden(first, starts, b)
        else:
            d, kind = (b - 3) // 2 + 1, (b - 3) % 2
            ref = (f1_ref, f2_ref, f3_ref)[d - 1]
            key, value = ref[kind, 0], ref[kind, 1]
            hidden = far_hidden(first, starts, behind(d, kind, x))
        pb, ds = pb_ref.at[b % 2], ds_ref.at[b % 2]
        for h in range(H):
            s = dot(key, head(q_ref, h), LONG)
            dp = dot(value, head(g_ref, h), LONG)
            s = jnp.where(hidden, NEG, s)
            pn = jnp.exp2((s - peak_ref[h : h + 1]) * TO_EXP2) * over_ref[h : h + 1]
            pb[h] = pn.astype(BF16)
            ds[h] = (pn * (dp - rd_ref[h : h + 1])).astype(BF16)
        kt, vt = key.T, value.T
        for h in range(H):
            o, dq = dot(vt, pb[h], PLAIN), dot(kt, ds[h], PLAIN)
            o_acc[h] = o if b == 0 else o_acc[h] + o
            dq_acc[h] = dq if b == 0 else dq_acc[h] + dq
        if b < 3:
            near_ref[b, 0], near_ref[b, 1] = key_side(q_ref, g_ref, pb, ds)

    for h in range(H):
        out_ref[:, h * D : (h + 1) * D] = o_acc[h].T.astype(BF16)
        dq_ref[:, h * D : (h + 1) * D] = dq_acc[h].T * SCALE


def gather_kernel(near_ref, g1_ref, g2_ref, g3_ref, own_ref, one_ref, two_ref):
    x = lax.rem(lax.axis_index("peer"), ROW)
    own, one, two = near_ref[0], near_ref[1], near_ref[2]
    for d, ref in enumerate((g1_ref, g2_ref, g3_ref), 1):
        a, b = ref[0].astype(F32), ref[1].astype(F32)
        same = x + d < ROW
        own += jnp.where(same, a, 0.0)
        two += jnp.where(same, 0.0, a)
        one += b
    own_ref[...] = own
    one_ref[...] = one.astype(BF16)
    two_ref[...] = two.astype(BF16)


def final_kernel(own_ref, one_ref, two_ref, dk_ref, dv_ref):
    dk_ref[...] = own_ref[0] + one_ref[0].astype(F32) + two_ref[0].astype(F32)
    dv_ref[...] = own_ref[1] + one_ref[1].astype(F32) + two_ref[1].astype(F32)


def along_z(block, rows, peers):
    far = rows * ROW
    return lax.ppermute(block, "peer", [(i, i + far) for i in range(peers) if 0 <= i + far < peers])


def along_x(block, columns, peers):
    return lax.ppermute(block, "peer", [(i, i - i % ROW + (i + columns) % ROW) for i in range(peers)])


def call(kernel, out, specs, scratch=(), blocks=0, limit=24, first=VM):
    return pl.pallas_call(
        kernel,
        out_shape=out,
        in_specs=specs,
        out_specs=(first,) + tuple(VM for _ in out[1:]),
        scratch_shapes=list(scratch),
        compiler_params=pltpu.CompilerParams(vmem_limit_bytes=limit << 20),
        cost_estimate=pl.CostEstimate(
            flops=blocks * H * T * T * D * 4, bytes_accessed=1 << 20, transcendentals=blocks * H * T * T
        ),
    )


def body(queries, keys, values, grad_out, doc_lengths):
    peers = lax.axis_size("peer")
    array = jax.ShapeDtypeStruct
    block, stats = (2, T, D), (H, T)
    pair = array((2, *block), BF16)
    tiles, sums = (array((2, H, T, T), F32),) * 2, (array((2, *stats), F32),) * 3
    staged = [pltpu.VMEM((2, H, T, T), BF16)] * 2
    (own,) = call(
        pair_kernel, (array(block, BF16),), [ANY] * 2, [pltpu.SemaphoreType.DMA((2,))], limit=60, first=ANY
    )(keys, values)
    z1 = along_z(own, 1, peers)
    z2 = along_z(own, 2, peers)
    wanted = (doc_lengths, queries, grad_out)
    (own,) = call(hold_kernel, (array(block, BF16),), [VM], limit=4)(own)
    packed = call(pack_kernel, (pair,) * 3, [VM] * 3, limit=4)(own, z1, z2)
    f1, f2, f3 = (along_x(p, d, peers) for d, p in enumerate(packed, 1))
    near = call(near_kernel, (array((3, *stats), F32),) * 3, [SM] + [VM] * 5, blocks=3, limit=8)(*wanted, own, z1, z2)
    tiles1, sums1, tiles3, sums3 = [], [], [], []
    for d, f, t, u in ((1, f1, tiles1, sums1), (3, f3, tiles3, sums3)):
        got = call(functools.partial(far_scores, d), tiles + sums, [SM] + [VM] * 3, blocks=2, limit=8)(*wanted, f)
        t.extend(got[:2])
        u.extend(got[2:])
    b2, peak, over, rd, w1, w3 = call(
        functools.partial(last_kernel, 2),
        (pair,) + (array(stats, F32),) * 3 + (array((2, *stats), F32),) * 2,
        [SM] + [VM] * 12,
        [pltpu.VMEM((2, H, T, T), F32)] * 2 + [pltpu.VMEM((2, *stats), F32)] * 4 + staged,
        blocks=4,
        limit=16,
    )(*wanted, f2, *near, *sums1, *sums3)
    r2 = along_x(b2, -2, peers)
    back = functools.partial(call, far_back, (pair,), [VM] * 6, staged, blocks=2, limit=8)
    (b3,) = back()(*tiles3, w3, rd, queries, grad_out)
    r3 = along_x(b3, -3, peers)
    (b1,) = back()(*tiles1, w1, rd, queries, grad_out)
    r1 = along_x(b1, -1, peers)
    attended, query_grad, mine = call(
        rest_kernel,
        (array((T, H * D), BF16), array((T, H * D), F32), array((3, *block), F32)),
        [SM] + [VM] * 11,
        [pltpu.VMEM((H, D, T), F32)] * 2 + staged,
        blocks=9,
        limit=16,
    )(*wanted, own, z1, z2, f1, f2, f3, peak, over, rd)
    mine, one, two = call(
        gather_kernel, (array(block, F32), array(block, BF16), array(block, BF16)), [VM] * 4, limit=8
    )(mine, r1, r2, r3)
    key_grad, value_grad = call(final_kernel, (array((T, D), F32),) * 2, [VM] * 3, limit=4)(
        mine, along_z(one, -1, peers), along_z(two, -2, peers)
    )
    return attended, query_grad, key_grad, value_grad


def solution(mesh):
    tokens = P("peer", "head")
    return jax.shard_map(
        body,
        mesh=mesh,
        in_specs=(tokens, tokens, tokens, tokens, P()),
        out_specs=(tokens, tokens, tokens, tokens),
        check_vma=False,
    )
```

```python
import functools
import math

import jax
import jax.numpy as jnp
from jax import lax
from jax.experimental import pallas as pl
from jax.experimental.pallas import tpu as pltpu
from jax.sharding import PartitionSpec as P

T = 256
D = 128
H = 4
ROW = 4
F32 = jnp.float32
BF16 = jnp.bfloat16
NEG = -1e30
SCALE = D**-0.5
TO_EXP2 = SCALE * math.log2(math.e)
LONG = (((1,), (1,)), ((), ()))
PLAIN = (((1,), (0,)), ((), ()))
VM = pl.BlockSpec(memory_space=pltpu.VMEM)
ANY = pl.BlockSpec(memory_space=pl.ANY)
SM = pl.BlockSpec(memory_space=pltpu.SMEM)


def dot(a, b, dims):
    return lax.dot_general(a, b, dims, preferred_element_type=F32)


def head(ref, h):
    return ref[:, h * D : (h + 1) * D]


def doc_starts(lengths_ref, first):
    place = first + lax.broadcasted_iota(jnp.int32, (1, T), 1)
    start = jnp.int32(0)
    own = jnp.zeros((1, T), jnp.int32)
    for i in range(lengths_ref.shape[0]):
        own = jnp.where(place >= start, start, own)
        start = start + lengths_ref[i]
    return own


def scores(q_ref, g_ref, key, value, hidden, index, m_ref, t_ref, r_ref, p_ref=None, dp_ref=None):
    for h in range(H):
        s = dot(key, head(q_ref, h), LONG)
        dp = dot(value, head(g_ref, h), LONG)
        s = jnp.where(hidden, NEG, s)
        m = jnp.max(s, axis=0, keepdims=True)
        p = jnp.exp2((s - m) * TO_EXP2)
        if p_ref is not None:
            p_ref[index, h] = p
            dp_ref[index, h] = dp
        m_ref[index, h : h + 1] = m
        t_ref[index, h : h + 1] = jnp.sum(p, axis=0, keepdims=True)
        r_ref[index, h : h + 1] = jnp.sum(p * dp, axis=0, keepdims=True)


def pair_kernel(k_ref, v_ref, out_ref):
    out_ref[0] = k_ref[...]
    out_ref[1] = v_ref[...]


def hold_kernel(lengths_ref, q_ref, g_ref, q_out, g_out, starts_ref):
    q_out[...] = q_ref[...]
    g_out[...] = g_ref[...]
    starts_ref[...] = doc_starts(lengths_ref, lax.axis_index("peer") * T)


def pack_kernel(_, own_ref, z1_ref, z2_ref, *out_refs):
    x = lax.rem(lax.axis_index("peer"), ROW)
    for d, ref in enumerate(out_refs, 1):

        @pl.when(x + d < ROW)
        def _(ref=ref):
            ref[0] = own_ref[...]

        @pl.when(x + d >= ROW)
        def _(ref=ref):
            ref[0] = z2_ref[...]

        ref[1] = z1_ref[...]


def near_hidden(first, starts, block):
    rows = lax.broadcasted_iota(jnp.int32, (T, 1), 0)
    hidden = (rows + (first - block * ROW * T)) < starts
    if block == 0:
        hidden = hidden | (rows > lax.broadcasted_iota(jnp.int32, (1, T), 1))
    return hidden


def far_hidden(first, starts, behind):
    rows = lax.broadcasted_iota(jnp.int32, (T, 1), 0)
    return (rows + (first - behind * T)) < starts


def near_kernel(starts_ref, q_ref, g_ref, own_ref, z1_ref, z2_ref, m_ref, t_ref, r_ref):
    first = lax.axis_index("peer") * T
    starts = starts_ref[...]
    for i, ref in enumerate((own_ref, z1_ref, z2_ref)):
        scores(q_ref, g_ref, ref[0], ref[1], near_hidden(first, starts, i), i, m_ref, t_ref, r_ref)


def behind(d, kind, x):
    return jnp.where((x >= d) ^ (kind == 1), d, ROW + d)


def key_side(q_ref, g_ref, pb_ref, ds_ref):
    dk = sum(dot(ds_ref[h], head(q_ref, h), PLAIN) for h in range(H))
    dv = sum(dot(pb_ref[h], head(g_ref, h), PLAIN) for h in range(H))
    return dk * SCALE, dv


def far_scores(d, starts_ref, q_ref, g_ref, far_ref, p_ref, dp_ref, m_ref, t_ref, r_ref):
    peer = lax.axis_index("peer")
    first = peer * T
    starts = starts_ref[...]
    for i in range(2):
        hidden = far_hidden(first, starts, behind(d, i, lax.rem(peer, ROW)))
        scores(q_ref, g_ref, far_ref[i, 0], far_ref[i, 1], hidden, i, m_ref, t_ref, r_ref, p_ref, dp_ref)


def far_back(p_ref, dp_ref, w_ref, rd_ref, q_ref, g_ref, back_ref, pb_ref, ds_ref):
    for i in range(2):
        for h in range(H):
            pn = p_ref[i, h] * w_ref[i, h : h + 1]
            pb_ref[i, h] = pn.astype(BF16)
            ds_ref[i, h] = (pn * (dp_ref[i, h] - rd_ref[h : h + 1])).astype(BF16)
        dk, dv = key_side(q_ref, g_ref, pb_ref.at[i], ds_ref.at[i])
        back_ref[i, 0] = dk.astype(BF16)
        back_ref[i, 1] = dv.astype(BF16)


def last_kernel(
    starts_ref, q_ref, g_ref, far_ref, mn, tn, rn, m1, t1, r1, p2_ref, dp2_ref, m2, t2, r2,
    back_ref, peak_ref, over_ref, rd_ref, w1_ref, w3_ref, p_ref, dp_ref,
    m_ref, t_ref, r_ref, w2_ref, pb_ref, ds_ref,
):
    far_scores(3, starts_ref, q_ref, g_ref, far_ref, p_ref, dp_ref, m_ref, t_ref, r_ref)

    def each(near, *pairs):
        return [near[b] for b in range(3)] + [ref[b] for ref in pairs for b in range(2)]

    peaks, totals, dots = each(mn, m1, m2, m_ref), each(tn, t1, t2, t_ref), each(rn, r1, r2, r_ref)
    peak = functools.reduce(jnp.maximum, peaks)
    factors = [jnp.exp2((m - peak) * TO_EXP2) for m in peaks]
    over = 1.0 / sum(f * t for f, t in zip(factors, totals))
    peak_ref[...] = peak
    over_ref[...] = over
    rd_ref[...] = sum(f * r for f, r in zip(factors, dots)) * over
    for n, ref in enumerate((w1_ref, w2_ref, w3_ref)):
        for b in range(2):
            ref[b] = factors[3 + 2 * n + b] * over
    far_back(p2_ref, dp2_ref, w2_ref, rd_ref, q_ref, g_ref, back_ref, pb_ref, ds_ref)


def rest_kernel(
    starts_ref, q_ref, g_ref, own_ref, z1_ref, z2_ref, f1_ref, f2_ref, f3_ref, peak_ref, over_ref, rd_ref,
    out_ref, dq_ref, near_ref, o_acc, dq_acc, pb_ref, ds_ref,
):
    peer = lax.axis_index("peer")
    x = lax.rem(peer, ROW)
    first = peer * T
    starts = starts_ref[...]
    near = (own_ref, z1_ref, z2_ref)
    for b in range(9):
        if b < 3:
            key, value = near[b][0], near[b][1]
            hidden = near_hidden(first, starts, b)
        else:
            d, kind = (b - 3) // 2 + 1, (b - 3) % 2
            ref = (f1_ref, f2_ref, f3_ref)[d - 1]
            key, value = ref[kind, 0], ref[kind, 1]
            hidden = far_hidden(first, starts, behind(d, kind, x))
        pb, ds = pb_ref.at[b % 2], ds_ref.at[b % 2]
        for h in range(H):
            s = dot(key, head(q_ref, h), LONG)
            dp = dot(value, head(g_ref, h), LONG)
            s = jnp.where(hidden, NEG, s)
            pn = jnp.exp2((s - peak_ref[h : h + 1]) * TO_EXP2) * over_ref[h : h + 1]
            pb[h] = pn.astype(BF16)
            ds[h] = (pn * (dp - rd_ref[h : h + 1])).astype(BF16)
        kt, vt = key.T, value.T
        for h in range(H):
            o, dq = dot(vt, pb[h], PLAIN), dot(kt, ds[h], PLAIN)
            o_acc[h] = o if b == 0 else o_acc[h] + o
            dq_acc[h] = dq if b == 0 else dq_acc[h] + dq
        if b < 3:
            near_ref[b, 0], near_ref[b, 1] = key_side(q_ref, g_ref, pb, ds)

    for h in range(H):
        out_ref[:, h * D : (h + 1) * D] = o_acc[h].T.astype(BF16)
        dq_ref[:, h * D : (h + 1) * D] = dq_acc[h].T * SCALE


def add_back(d, ref, own, one, two):
    same = lax.rem(lax.axis_index("peer"), ROW) + d < ROW
    a, b = ref[0].astype(F32), ref[1].astype(F32)
    return own + jnp.where(same, a, 0.0), one + b, two + jnp.where(same, 0.0, a)


def gather_first_kernel(mine_ref, r2_ref, out_ref):
    for i, total in enumerate(add_back(2, r2_ref, mine_ref[0], mine_ref[1], mine_ref[2])):
        out_ref[i] = total


def gather_kernel(mine_ref, r1_ref, r3_ref, own_ref, one_ref, two_ref):
    own, one, two = add_back(3, r3_ref, *add_back(1, r1_ref, mine_ref[0], mine_ref[1], mine_ref[2]))
    own_ref[...] = own
    one_ref[...] = one.astype(BF16)
    two_ref[...] = two.astype(BF16)


def add_two_kernel(own_ref, two_ref, out_ref):
    out_ref[...] = own_ref[...] + two_ref[...].astype(F32)


def final_kernel(own_ref, one_ref, dk_ref, dv_ref):
    dk_ref[...] = own_ref[0] + one_ref[0].astype(F32)
    dv_ref[...] = own_ref[1] + one_ref[1].astype(F32)


def along_z(block, rows, peers):
    far = rows * ROW
    return lax.ppermute(block, "peer", [(i, i + far) for i in range(peers) if 0 <= i + far < peers])


def along_x(block, columns, peers):
    return lax.ppermute(block, "peer", [(i, i - i % ROW + (i + columns) % ROW) for i in range(peers)])


def call(kernel, out, specs, scratch=(), blocks=0, limit=24, first=VM):
    return pl.pallas_call(
        kernel,
        out_shape=out,
        in_specs=specs,
        out_specs=(first,) + tuple(VM for _ in out[1:]),
        scratch_shapes=list(scratch),
        compiler_params=pltpu.CompilerParams(vmem_limit_bytes=limit << 20),
        cost_estimate=pl.CostEstimate(
            flops=blocks * H * T * T * D * 4, bytes_accessed=1 << 20, transcendentals=blocks * H * T * T
        ),
    )


def body(queries, keys, values, grad_out, doc_lengths):
    peers = lax.axis_size("peer")
    array = jax.ShapeDtypeStruct
    block, stats = (2, T, D), (H, T)
    pair = array((2, *block), BF16)
    tiles, sums = (array((2, H, T, T), F32),) * 2, (array((2, *stats), F32),) * 3
    staged = [pltpu.VMEM((2, H, T, T), BF16)] * 2
    (own,) = call(pair_kernel, (array(block, BF16),), [VM] * 2, limit=4)(keys, values)
    z1 = along_z(own, 1, peers)
    z2 = along_z(own, 2, peers)
    queries, grad_out, starts = call(
        hold_kernel,
        (array((T, H * D), BF16), array((T, H * D), BF16), array((1, T), jnp.int32)),
        [SM] + [VM] * 2,
        blocks=1,
        limit=4,
    )(doc_lengths, queries, grad_out)
    wanted = (starts, queries, grad_out)
    packed = call(pack_kernel, (pair,) * 3, [VM] * 4, limit=4)(starts, own, z1, z2)
    f1, f2, f3 = (along_x(p, d, peers) for d, p in enumerate(packed, 1))
    near = call(near_kernel, (array((3, *stats), F32),) * 3, [VM] * 6, blocks=3, limit=8)(*wanted, own, z1, z2)
    arrive = {d: call(functools.partial(far_scores, d), tiles + sums, [VM] * 4, blocks=2, limit=8) for d in (1, 2)}
    p2, dp2, *sums2 = arrive[2](*wanted, f2)
    p1, dp1, *sums1 = arrive[1](*wanted, f1)
    b2, peak, over, rd, w1, w3, p3, dp3 = call(
        last_kernel,
        (pair,) + (array(stats, F32),) * 3 + (array((2, *stats), F32),) * 2 + tiles,
        [VM] * 15,
        [pltpu.VMEM((2, *stats), F32)] * 4 + staged,
        blocks=4,
        limit=8,
    )(*wanted, f3, *near, *sums1, p2, dp2, *sums2)
    r2 = along_x(b2, -2, peers)
    back = functools.partial(call, far_back, (pair,), [VM] * 6, staged, blocks=2, limit=8)
    (b3,) = back()(p3, dp3, w3, rd, queries, grad_out)
    r3 = along_x(b3, -3, peers)
    (b1,) = back()(p1, dp1, w1, rd, queries, grad_out)
    r1 = along_x(b1, -1, peers)
    attended, query_grad, mine = call(
        rest_kernel,
        (array((T, H * D), BF16), array((T, H * D), F32), array((3, *block), F32)),
        [VM] * 12,
        [pltpu.VMEM((H, D, T), F32)] * 2 + staged,
        blocks=9,
        limit=16,
    )(*wanted, own, z1, z2, f1, f2, f3, peak, over, rd)
    (mine,) = call(gather_first_kernel, (array((3, *block), F32),), [VM] * 2, limit=4)(mine, r2)
    mine, one, two = call(
        gather_kernel, (array(block, F32), array(block, BF16), array(block, BF16)), [VM] * 3, limit=4
    )(mine, r1, r3)
    two, one = along_z(two, -2, peers), along_z(one, -1, peers)
    (mine,) = call(add_two_kernel, (array(block, F32),), [VM] * 2, limit=4)(mine, two)
    key_grad, value_grad = call(final_kernel, (array((T, D), F32),) * 2, [VM] * 2, limit=4)(mine, one)
    return attended, query_grad, key_grad, value_grad


def solution(mesh):
    tokens = P("peer", "head")
    return jax.shard_map(
        body,
        mesh=mesh,
        in_specs=(tokens, tokens, tokens, tokens, P()),
        out_specs=(tokens, tokens, tokens, tokens),
        check_vma=False,
    )
```

```python
import functools
import math

import jax
import jax.numpy as jnp
from jax import lax
from jax.experimental import pallas as pl
from jax.experimental.pallas import tpu as pltpu
from jax.sharding import PartitionSpec as P

T = 256
D = 128
H = 4
ROW = 4
F32 = jnp.float32
BF16 = jnp.bfloat16
NEG = -1e30
SCALE = D**-0.5
TO_EXP2 = SCALE * math.log2(math.e)
LONG = (((1,), (1,)), ((), ()))
PLAIN = (((1,), (0,)), ((), ()))
VM = pl.BlockSpec(memory_space=pltpu.VMEM)
ANY = pl.BlockSpec(memory_space=pl.ANY)
SM = pl.BlockSpec(memory_space=pltpu.SMEM)


def dot(a, b, dims):
    return lax.dot_general(a, b, dims, preferred_element_type=F32)


def head(ref, h):
    return ref[:, h * D : (h + 1) * D]


def doc_starts(lengths_ref, first):
    place = first + lax.broadcasted_iota(jnp.int32, (1, T), 1)
    start = jnp.int32(0)
    own = jnp.zeros((1, T), jnp.int32)
    for i in range(lengths_ref.shape[0]):
        own = jnp.where(place >= start, start, own)
        start = start + lengths_ref[i]
    return own


def scores(q_ref, g_ref, key, value, hidden, index, m_ref, t_ref, r_ref, p_ref=None, dp_ref=None):
    for h in range(H):
        s = dot(key, head(q_ref, h), LONG)
        dp = dot(value, head(g_ref, h), LONG)
        s = jnp.where(hidden, NEG, s)
        m = jnp.max(s, axis=0, keepdims=True)
        p = jnp.exp2((s - m) * TO_EXP2)
        if p_ref is not None:
            p_ref[index, h] = p
            dp_ref[index, h] = dp
        m_ref[index, h : h + 1] = m
        t_ref[index, h : h + 1] = jnp.sum(p, axis=0, keepdims=True)
        r_ref[index, h : h + 1] = jnp.sum(p * dp, axis=0, keepdims=True)


def pair_kernel(k_ref, v_ref, out_ref):
    out_ref[0] = k_ref[...]
    out_ref[1] = v_ref[...]


def hold_kernel(lengths_ref, q_ref, g_ref, q_out, g_out, starts_ref):
    q_out[...] = q_ref[...]
    g_out[...] = g_ref[...]
    starts_ref[...] = doc_starts(lengths_ref, lax.axis_index("peer") * T)


def pack_kernel(_, own_ref, z1_ref, z2_ref, *out_refs):
    x = lax.rem(lax.axis_index("peer"), ROW)
    for d, ref in enumerate(out_refs, 1):

        @pl.when(x + d < ROW)
        def _(ref=ref):
            ref[0] = own_ref[...]

        @pl.when(x + d >= ROW)
        def _(ref=ref):
            ref[0] = z2_ref[...]

        ref[1] = z1_ref[...]


def near_hidden(first, starts, block):
    rows = lax.broadcasted_iota(jnp.int32, (T, 1), 0)
    hidden = (rows + (first - block * ROW * T)) < starts
    if block == 0:
        hidden = hidden | (rows > lax.broadcasted_iota(jnp.int32, (1, T), 1))
    return hidden


def far_hidden(first, starts, behind):
    rows = lax.broadcasted_iota(jnp.int32, (T, 1), 0)
    return (rows + (first - behind * T)) < starts


def near_kernel(starts_ref, q_ref, g_ref, own_ref, z1_ref, z2_ref, m_ref, t_ref, r_ref):
    first = lax.axis_index("peer") * T
    starts = starts_ref[...]
    for i, ref in enumerate((own_ref, z1_ref, z2_ref)):
        scores(q_ref, g_ref, ref[0], ref[1], near_hidden(first, starts, i), i, m_ref, t_ref, r_ref)


def behind(d, kind, x):
    return jnp.where((x >= d) ^ (kind == 1), d, ROW + d)


def key_side(q_ref, g_ref, pb_ref, ds_ref):
    dk = sum(dot(ds_ref[h], head(q_ref, h), PLAIN) for h in range(H))
    dv = sum(dot(pb_ref[h], head(g_ref, h), PLAIN) for h in range(H))
    return dk * SCALE, dv


def far_scores(d, starts_ref, q_ref, g_ref, far_ref, p_ref, dp_ref, m_ref, t_ref, r_ref):
    peer = lax.axis_index("peer")
    first = peer * T
    starts = starts_ref[...]
    for i in range(2):
        hidden = far_hidden(first, starts, behind(d, i, lax.rem(peer, ROW)))
        scores(q_ref, g_ref, far_ref[i, 0], far_ref[i, 1], hidden, i, m_ref, t_ref, r_ref, p_ref, dp_ref)


def far_back(p_ref, dp_ref, w_ref, rd_ref, q_ref, g_ref, back_ref, pb_ref, ds_ref):
    for i in range(2):
        for h in range(H):
            pn = p_ref[i, h] * w_ref[i, h : h + 1]
            pb_ref[i, h] = pn.astype(BF16)
            ds_ref[i, h] = (pn * (dp_ref[i, h] - rd_ref[h : h + 1])).astype(BF16)
        dk, dv = key_side(q_ref, g_ref, pb_ref.at[i], ds_ref.at[i])
        back_ref[i, 0] = dk.astype(BF16)
        back_ref[i, 1] = dv.astype(BF16)


def last_kernel(
    starts_ref, q_ref, g_ref, far_ref, mn, tn, rn, p1_ref, dp1_ref, m1, t1, r1, p2_ref, dp2_ref, m2, t2, r2,
    b1_ref, b2_ref, b3_ref, peak_ref, over_ref, rd_ref,
    p3_ref, dp3_ref, m_ref, t_ref, r_ref, w1_ref, w2_ref, w3_ref, pb_ref, ds_ref,
):
    far_scores(3, starts_ref, q_ref, g_ref, far_ref, p3_ref, dp3_ref, m_ref, t_ref, r_ref)

    def each(near, *pairs):
        return [near[b] for b in range(3)] + [ref[b] for ref in pairs for b in range(2)]

    peaks, totals, dots = each(mn, m1, m2, m_ref), each(tn, t1, t2, t_ref), each(rn, r1, r2, r_ref)
    peak = functools.reduce(jnp.maximum, peaks)
    factors = [jnp.exp2((m - peak) * TO_EXP2) for m in peaks]
    over = 1.0 / sum(f * t for f, t in zip(factors, totals))
    peak_ref[...] = peak
    over_ref[...] = over
    rd_ref[...] = sum(f * r for f, r in zip(factors, dots)) * over
    for n, ref in enumerate((w1_ref, w2_ref, w3_ref)):
        for b in range(2):
            ref[b] = factors[3 + 2 * n + b] * over
    far_back(p2_ref, dp2_ref, w2_ref, rd_ref, q_ref, g_ref, b2_ref, pb_ref, ds_ref)
    far_back(p1_ref, dp1_ref, w1_ref, rd_ref, q_ref, g_ref, b1_ref, pb_ref, ds_ref)
    far_back(p3_ref, dp3_ref, w3_ref, rd_ref, q_ref, g_ref, b3_ref, pb_ref, ds_ref)


def rest_kernel(
    starts_ref, q_ref, g_ref, own_ref, z1_ref, z2_ref, f1_ref, f2_ref, f3_ref, peak_ref, over_ref, rd_ref,
    out_ref, dq_ref, near_ref, o_acc, dq_acc, pb_ref, ds_ref,
):
    peer = lax.axis_index("peer")
    x = lax.rem(peer, ROW)
    first = peer * T
    starts = starts_ref[...]
    near = (own_ref, z1_ref, z2_ref)
    for b in range(9):
        if b < 3:
            key, value = near[b][0], near[b][1]
            hidden = near_hidden(first, starts, b)
        else:
            d, kind = (b - 3) // 2 + 1, (b - 3) % 2
            ref = (f1_ref, f2_ref, f3_ref)[d - 1]
            key, value = ref[kind, 0], ref[kind, 1]
            hidden = far_hidden(first, starts, behind(d, kind, x))
        pb, ds = pb_ref.at[b % 2], ds_ref.at[b % 2]
        for h in range(H):
            s = dot(key, head(q_ref, h), LONG)
            dp = dot(value, head(g_ref, h), LONG)
            s = jnp.where(hidden, NEG, s)
            pn = jnp.exp2((s - peak_ref[h : h + 1]) * TO_EXP2) * over_ref[h : h + 1]
            pb[h] = pn.astype(BF16)
            ds[h] = (pn * (dp - rd_ref[h : h + 1])).astype(BF16)
        kt, vt = key.T, value.T
        for h in range(H):
            o, dq = dot(vt, pb[h], PLAIN), dot(kt, ds[h], PLAIN)
            o_acc[h] = o if b == 0 else o_acc[h] + o
            dq_acc[h] = dq if b == 0 else dq_acc[h] + dq
        if b < 3:
            near_ref[b, 0], near_ref[b, 1] = key_side(q_ref, g_ref, pb, ds)

    for h in range(H):
        out_ref[:, h * D : (h + 1) * D] = o_acc[h].T.astype(BF16)
        dq_ref[:, h * D : (h + 1) * D] = dq_acc[h].T * SCALE


def add_back(d, ref, own, one, two):
    same = lax.rem(lax.axis_index("peer"), ROW) + d < ROW
    a, b = ref[0].astype(F32), ref[1].astype(F32)
    return own + jnp.where(same, a, 0.0), one + b, two + jnp.where(same, 0.0, a)


def gather_first_kernel(mine_ref, r2_ref, out_ref):
    for i, total in enumerate(add_back(2, r2_ref, mine_ref[0], mine_ref[1], mine_ref[2])):
        out_ref[i] = total


def gather_one_kernel(mine_ref, r1_ref, out_ref):
    for i, total in enumerate(add_back(1, r1_ref, mine_ref[0], mine_ref[1], mine_ref[2])):
        out_ref[i] = total


def gather_kernel(mine_ref, r3_ref, own_ref, one_ref, two_ref):
    own, one, two = add_back(3, r3_ref, mine_ref[0], mine_ref[1], mine_ref[2])
    own_ref[...] = own
    one_ref[...] = one.astype(BF16)
    two_ref[...] = two.astype(BF16)


def add_two_kernel(own_ref, two_ref, out_ref):
    out_ref[...] = own_ref[...] + two_ref[...].astype(F32)


def final_kernel(own_ref, one_ref, dk_ref, dv_ref):
    dk_ref[...] = own_ref[0] + one_ref[0].astype(F32)
    dv_ref[...] = own_ref[1] + one_ref[1].astype(F32)


def along_z(block, rows, peers):
    far = rows * ROW
    return lax.ppermute(block, "peer", [(i, i + far) for i in range(peers) if 0 <= i + far < peers])


def along_x(block, columns, peers):
    return lax.ppermute(block, "peer", [(i, i - i % ROW + (i + columns) % ROW) for i in range(peers)])


def call(kernel, out, specs, scratch=(), blocks=0, limit=24, first=VM):
    return pl.pallas_call(
        kernel,
        out_shape=out,
        in_specs=specs,
        out_specs=(first,) + tuple(VM for _ in out[1:]),
        scratch_shapes=list(scratch),
        compiler_params=pltpu.CompilerParams(vmem_limit_bytes=limit << 20),
        cost_estimate=pl.CostEstimate(
            flops=blocks * H * T * T * D * 4, bytes_accessed=1 << 20, transcendentals=blocks * H * T * T
        ),
    )


def body(queries, keys, values, grad_out, doc_lengths):
    peers = lax.axis_size("peer")
    array = jax.ShapeDtypeStruct
    block, stats = (2, T, D), (H, T)
    pair = array((2, *block), BF16)
    tiles, sums = (array((2, H, T, T), F32),) * 2, (array((2, *stats), F32),) * 3
    staged = [pltpu.VMEM((2, H, T, T), BF16)] * 2
    (own,) = call(pair_kernel, (array(block, BF16),), [VM] * 2, limit=4)(keys, values)
    z1 = along_z(own, 1, peers)
    z2 = along_z(own, 2, peers)
    queries, grad_out, starts = call(
        hold_kernel,
        (array((T, H * D), BF16), array((T, H * D), BF16), array((1, T), jnp.int32)),
        [SM] + [VM] * 2,
        blocks=1,
        limit=4,
    )(doc_lengths, queries, grad_out)
    wanted = (starts, queries, grad_out)
    packed = call(pack_kernel, (pair,) * 3, [VM] * 4, limit=4)(starts, own, z1, z2)
    f1, f2, f3 = (along_x(p, d, peers) for d, p in enumerate(packed, 1))
    near = call(near_kernel, (array((3, *stats), F32),) * 3, [VM] * 6, blocks=3, limit=8)(*wanted, own, z1, z2)
    arrive = {d: call(functools.partial(far_scores, d), tiles + sums, [VM] * 4, blocks=2, limit=8) for d in (1, 2)}
    p2, dp2, *sums2 = arrive[2](*wanted, f2)
    p1, dp1, *sums1 = arrive[1](*wanted, f1)
    *backs, peak, over, rd = call(
        last_kernel,
        (pair,) * 3 + (array(stats, F32),) * 3,
        [VM] * 17,
        [pltpu.VMEM((2, H, T, T), F32)] * 2 + [pltpu.VMEM((2, *stats), F32)] * 6 + staged,
        blocks=8,
        limit=16,
    )(*wanted, f3, *near, p1, dp1, *sums1, p2, dp2, *sums2)
    r1, r2, r3 = (along_x(b, -d, peers) for d, b in enumerate(backs, 1))
    attended, query_grad, mine = call(
        rest_kernel,
        (array((T, H * D), BF16), array((T, H * D), F32), array((3, *block), F32)),
        [VM] * 12,
        [pltpu.VMEM((H, D, T), F32)] * 2 + staged,
        blocks=9,
        limit=16,
    )(*wanted, own, z1, z2, f1, f2, f3, peak, over, rd)
    (mine,) = call(gather_first_kernel, (array((3, *block), F32),), [VM] * 2, limit=4)(mine, r2)
    (mine,) = call(gather_one_kernel, (array((3, *block), F32),), [VM] * 2, limit=4)(mine, r1)
    mine, one, two = call(
        gather_kernel, (array(block, F32), array(block, BF16), array(block, BF16)), [VM] * 2, limit=4
    )(mine, r3)
    two, one = along_z(two, -2, peers), along_z(one, -1, peers)
    (mine,) = call(add_two_kernel, (array(block, F32),), [VM] * 2, limit=4)(mine, two)
    key_grad, value_grad = call(final_kernel, (array((T, D), F32),) * 2, [VM] * 2, limit=4)(mine, one)
    return attended, query_grad, key_grad, value_grad


def solution(mesh):
    tokens = P("peer", "head")
    return jax.shard_map(
        body,
        mesh=mesh,
        in_specs=(tokens, tokens, tokens, tokens, P()),
        out_specs=(tokens, tokens, tokens, tokens),
        check_vma=False,
    )
```

```python
import functools
import math

import jax
import jax.numpy as jnp
from jax import lax
from jax.experimental import pallas as pl
from jax.experimental.pallas import tpu as pltpu
from jax.sharding import PartitionSpec as P

T = 256
D = 128
H = 4
ROW = 4
F32 = jnp.float32
BF16 = jnp.bfloat16
NEG = -1e30
SCALE = D**-0.5
TO_EXP2 = SCALE * math.log2(math.e)
LONG = (((1,), (1,)), ((), ()))
PLAIN = (((1,), (0,)), ((), ()))
VM = pl.BlockSpec(memory_space=pltpu.VMEM)
ANY = pl.BlockSpec(memory_space=pl.ANY)
SM = pl.BlockSpec(memory_space=pltpu.SMEM)


def dot(a, b, dims):
    return lax.dot_general(a, b, dims, preferred_element_type=F32)


def head(ref, h):
    return ref[:, h * D : (h + 1) * D]


def doc_starts(lengths_ref, first):
    place = first + lax.broadcasted_iota(jnp.int32, (1, T), 1)
    start = jnp.int32(0)
    own = jnp.zeros((1, T), jnp.int32)
    for i in range(lengths_ref.shape[0]):
        own = jnp.where(place >= start, start, own)
        start = start + lengths_ref[i]
    return own


def scores(q_ref, g_ref, key, value, hidden, index, m_ref, t_ref, r_ref, p_ref=None, dp_ref=None):
    for h in range(H):
        s = dot(key, head(q_ref, h), LONG)
        dp = dot(value, head(g_ref, h), LONG)
        s = jnp.where(hidden, NEG, s)
        m = jnp.max(s, axis=0, keepdims=True)
        p = jnp.exp2((s - m) * TO_EXP2)
        if p_ref is not None:
            p_ref[index, h] = p
            dp_ref[index, h] = dp
        m_ref[index, h : h + 1] = m
        t_ref[index, h : h + 1] = jnp.sum(p, axis=0, keepdims=True)
        r_ref[index, h : h + 1] = jnp.sum(p * dp, axis=0, keepdims=True)


def pair_kernel(k_ref, v_ref, out_ref):
    out_ref[0] = k_ref[...]
    out_ref[1] = v_ref[...]


def hold_kernel(lengths_ref, q_ref, g_ref, q_out, g_out, starts_ref):
    q_out[...] = q_ref[...]
    g_out[...] = g_ref[...]
    starts_ref[...] = doc_starts(lengths_ref, lax.axis_index("peer") * T)


def pack_kernel(_, own_ref, z1_ref, z2_ref, *out_refs):
    x = lax.rem(lax.axis_index("peer"), ROW)
    for d, ref in enumerate(out_refs, 1):

        @pl.when(x + d < ROW)
        def _(ref=ref):
            ref[0] = own_ref[...]

        @pl.when(x + d >= ROW)
        def _(ref=ref):
            ref[0] = z2_ref[...]

        ref[1] = z1_ref[...]


def near_hidden(first, starts, block):
    rows = lax.broadcasted_iota(jnp.int32, (T, 1), 0)
    hidden = (rows + (first - block * ROW * T)) < starts
    if block == 0:
        hidden = hidden | (rows > lax.broadcasted_iota(jnp.int32, (1, T), 1))
    return hidden


def far_hidden(first, starts, behind):
    rows = lax.broadcasted_iota(jnp.int32, (T, 1), 0)
    return (rows + (first - behind * T)) < starts


def near_kernel(starts_ref, q_ref, g_ref, own_ref, z1_ref, z2_ref, m_ref, t_ref, r_ref):
    first = lax.axis_index("peer") * T
    starts = starts_ref[...]
    for i, ref in enumerate((own_ref, z1_ref, z2_ref)):
        scores(q_ref, g_ref, ref[0], ref[1], near_hidden(first, starts, i), i, m_ref, t_ref, r_ref)


def behind(d, kind, x):
    return jnp.where((x >= d) ^ (kind == 1), d, ROW + d)


def key_side(q_ref, g_ref, pb_ref, ds_ref):
    dk = sum(dot(ds_ref[h], head(q_ref, h), PLAIN) for h in range(H))
    dv = sum(dot(pb_ref[h], head(g_ref, h), PLAIN) for h in range(H))
    return dk * SCALE, dv


def far_scores(d, starts_ref, q_ref, g_ref, far_ref, p_ref, dp_ref, m_ref, t_ref, r_ref):
    peer = lax.axis_index("peer")
    first = peer * T
    starts = starts_ref[...]
    for i in range(2):
        hidden = far_hidden(first, starts, behind(d, i, lax.rem(peer, ROW)))
        scores(q_ref, g_ref, far_ref[i, 0], far_ref[i, 1], hidden, i, m_ref, t_ref, r_ref, p_ref, dp_ref)


def far_back(p_ref, dp_ref, w_ref, rd_ref, q_ref, g_ref, back_ref, pb_ref, ds_ref):
    for i in range(2):
        for h in range(H):
            pn = p_ref[i, h] * w_ref[i, h : h + 1]
            pb_ref[i, h] = pn.astype(BF16)
            ds_ref[i, h] = (pn * (dp_ref[i, h] - rd_ref[h : h + 1])).astype(BF16)
        dk, dv = key_side(q_ref, g_ref, pb_ref.at[i], ds_ref.at[i])
        back_ref[i, 0] = dk.astype(BF16)
        back_ref[i, 1] = dv.astype(BF16)


def last_kernel(
    starts_ref, q_ref, g_ref, far_ref, mn, tn, rn, p1_ref, dp1_ref, m1, t1, r1, p2_ref, dp2_ref, m2, t2, r2,
    b1_ref, b2_ref, b3_ref, peak_ref, over_ref, rd_ref,
    p3_ref, dp3_ref, m_ref, t_ref, r_ref, w1_ref, w2_ref, w3_ref, pb_ref, ds_ref,
):
    far_scores(3, starts_ref, q_ref, g_ref, far_ref, p3_ref, dp3_ref, m_ref, t_ref, r_ref)

    def each(near, *pairs):
        return [near[b] for b in range(3)] + [ref[b] for ref in pairs for b in range(2)]

    peaks, totals, dots = each(mn, m1, m2, m_ref), each(tn, t1, t2, t_ref), each(rn, r1, r2, r_ref)
    peak = functools.reduce(jnp.maximum, peaks)
    factors = [jnp.exp2((m - peak) * TO_EXP2) for m in peaks]
    over = 1.0 / sum(f * t for f, t in zip(factors, totals))
    peak_ref[...] = peak
    over_ref[...] = over
    rd_ref[...] = sum(f * r for f, r in zip(factors, dots)) * over
    for n, ref in enumerate((w1_ref, w2_ref, w3_ref)):
        for b in range(2):
            ref[b] = factors[3 + 2 * n + b] * over
    far_back(p2_ref, dp2_ref, w2_ref, rd_ref, q_ref, g_ref, b2_ref, pb_ref, ds_ref)
    far_back(p1_ref, dp1_ref, w1_ref, rd_ref, q_ref, g_ref, b1_ref, pb_ref, ds_ref)
    far_back(p3_ref, dp3_ref, w3_ref, rd_ref, q_ref, g_ref, b3_ref, pb_ref, ds_ref)


def weights(q_ref, g_ref, key, value, hidden, peak_ref, over_ref, rd_ref, pb_ref, ds_ref):
    for h in range(H):
        s = dot(key, head(q_ref, h), LONG)
        dp = dot(value, head(g_ref, h), LONG)
        s = jnp.where(hidden, NEG, s)
        pn = jnp.exp2((s - peak_ref[h : h + 1]) * TO_EXP2) * over_ref[h : h + 1]
        pb_ref[h] = pn.astype(BF16)
        ds_ref[h] = (pn * (dp - rd_ref[h : h + 1])).astype(BF16)


def near_back_kernel(starts_ref, q_ref, g_ref, own_ref, z1_ref, z2_ref, peak_ref, over_ref, rd_ref, near_ref, pb_ref, ds_ref):
    first = lax.axis_index("peer") * T
    for b, ref in enumerate((own_ref, z1_ref, z2_ref)):
        pb, ds = pb_ref.at[b % 2], ds_ref.at[b % 2]
        hidden = near_hidden(first, starts_ref[...], b)
        weights(q_ref, g_ref, ref[0], ref[1], hidden, peak_ref, over_ref, rd_ref, pb, ds)
        near_ref[b, 0], near_ref[b, 1] = key_side(q_ref, g_ref, pb, ds)


def query_side_kernel(
    starts_ref, q_ref, g_ref, own_ref, z1_ref, z2_ref, f1_ref, f2_ref, f3_ref, peak_ref, over_ref, rd_ref, _,
    out_ref, dq_ref, o_acc, dq_acc, pb_ref, ds_ref,
):
    peer = lax.axis_index("peer")
    x = lax.rem(peer, ROW)
    first = peer * T
    starts = starts_ref[...]
    near = (own_ref, z1_ref, z2_ref)
    for b in range(9):
        if b < 3:
            key, value = near[b][0], near[b][1]
            hidden = near_hidden(first, starts, b)
        else:
            d, kind = (b - 3) // 2 + 1, (b - 3) % 2
            ref = (f1_ref, f2_ref, f3_ref)[d - 1]
            key, value = ref[kind, 0], ref[kind, 1]
            hidden = far_hidden(first, starts, behind(d, kind, x))
        pb, ds = pb_ref.at[b % 2], ds_ref.at[b % 2]
        weights(q_ref, g_ref, key, value, hidden, peak_ref, over_ref, rd_ref, pb, ds)
        kt, vt = key.T, value.T
        for h in range(H):
            o, dq = dot(vt, pb[h], PLAIN), dot(kt, ds[h], PLAIN)
            o_acc[h] = o if b == 0 else o_acc[h] + o
            dq_acc[h] = dq if b == 0 else dq_acc[h] + dq

    for h in range(H):
        out_ref[:, h * D : (h + 1) * D] = o_acc[h].T.astype(BF16)
        dq_ref[:, h * D : (h + 1) * D] = dq_acc[h].T * SCALE


def add_back(d, ref, own, one, two):
    same = lax.rem(lax.axis_index("peer"), ROW) + d < ROW
    a, b = ref[0].astype(F32), ref[1].astype(F32)
    return own + jnp.where(same, a, 0.0), one + b, two + jnp.where(same, 0.0, a)


def gather_first_kernel(mine_ref, r2_ref, out_ref):
    for i, total in enumerate(add_back(2, r2_ref, mine_ref[0], mine_ref[1], mine_ref[2])):
        out_ref[i] = total


def gather_one_kernel(mine_ref, r1_ref, out_ref):
    for i, total in enumerate(add_back(1, r1_ref, mine_ref[0], mine_ref[1], mine_ref[2])):
        out_ref[i] = total


def gather_kernel(mine_ref, r3_ref, own_ref, one_ref, two_ref):
    own, one, two = add_back(3, r3_ref, mine_ref[0], mine_ref[1], mine_ref[2])
    own_ref[...] = own
    one_ref[...] = one.astype(BF16)
    two_ref[...] = two.astype(BF16)


def add_two_kernel(own_ref, two_ref, out_ref):
    out_ref[...] = own_ref[...] + two_ref[...].astype(F32)


def final_kernel(own_ref, one_ref, dk_ref, dv_ref):
    dk_ref[...] = own_ref[0] + one_ref[0].astype(F32)
    dv_ref[...] = own_ref[1] + one_ref[1].astype(F32)


def along_z(block, rows, peers):
    far = rows * ROW
    return lax.ppermute(block, "peer", [(i, i + far) for i in range(peers) if 0 <= i + far < peers])


def along_x(block, columns, peers):
    return lax.ppermute(block, "peer", [(i, i - i % ROW + (i + columns) % ROW) for i in range(peers)])


def call(kernel, out, specs, scratch=(), blocks=0, limit=24, first=VM):
    return pl.pallas_call(
        kernel,
        out_shape=out,
        in_specs=specs,
        out_specs=(first,) + tuple(VM for _ in out[1:]),
        scratch_shapes=list(scratch),
        compiler_params=pltpu.CompilerParams(vmem_limit_bytes=limit << 20),
        cost_estimate=pl.CostEstimate(
            flops=blocks * H * T * T * D * 4, bytes_accessed=1 << 20, transcendentals=blocks * H * T * T
        ),
    )


def body(queries, keys, values, grad_out, doc_lengths):
    peers = lax.axis_size("peer")
    array = jax.ShapeDtypeStruct
    block, stats = (2, T, D), (H, T)
    pair = array((2, *block), BF16)
    tiles, sums = (array((2, H, T, T), F32),) * 2, (array((2, *stats), F32),) * 3
    staged = [pltpu.VMEM((2, H, T, T), BF16)] * 2
    (own,) = call(pair_kernel, (array(block, BF16),), [VM] * 2, limit=4)(keys, values)
    z1 = along_z(own, 1, peers)
    z2 = along_z(own, 2, peers)
    queries, grad_out, starts = call(
        hold_kernel,
        (array((T, H * D), BF16), array((T, H * D), BF16), array((1, T), jnp.int32)),
        [SM] + [VM] * 2,
        blocks=1,
        limit=4,
    )(doc_lengths, queries, grad_out)
    wanted = (starts, queries, grad_out)
    packed = call(pack_kernel, (pair,) * 3, [VM] * 4, limit=4)(starts, own, z1, z2)
    f1, f2, f3 = (along_x(p, d, peers) for d, p in enumerate(packed, 1))
    near = call(near_kernel, (array((3, *stats), F32),) * 3, [VM] * 6, blocks=3, limit=8)(*wanted, own, z1, z2)
    arrive = {d: call(functools.partial(far_scores, d), tiles + sums, [VM] * 4, blocks=2, limit=8) for d in (1, 2)}
    p2, dp2, *sums2 = arrive[2](*wanted, f2)
    p1, dp1, *sums1 = arrive[1](*wanted, f1)
    *backs, peak, over, rd = call(
        last_kernel,
        (pair,) * 3 + (array(stats, F32),) * 3,
        [VM] * 17,
        [pltpu.VMEM((2, H, T, T), F32)] * 2 + [pltpu.VMEM((2, *stats), F32)] * 6 + staged,
        blocks=8,
        limit=16,
    )(*wanted, f3, *near, p1, dp1, *sums1, p2, dp2, *sums2)
    r1, r2, r3 = (along_x(b, -d, peers) for d, b in enumerate(backs, 1))
    (mine,) = call(near_back_kernel, (array((3, *block), F32),), [VM] * 9, staged, blocks=3, limit=8)(
        *wanted, own, z1, z2, peak, over, rd
    )
    (mine,) = call(gather_first_kernel, (array((3, *block), F32),), [VM] * 2, limit=4)(mine, r2)
    (mine,) = call(gather_one_kernel, (array((3, *block), F32),), [VM] * 2, limit=4)(mine, r1)
    mine, one, two = call(
        gather_kernel, (array(block, F32), array(block, BF16), array(block, BF16)), [VM] * 2, limit=4
    )(mine, r3)
    attended, query_grad = call(
        query_side_kernel,
        (array((T, H * D), BF16), array((T, H * D), F32)),
        [VM] * 13,
        [pltpu.VMEM((H, D, T), F32)] * 2 + staged,
        blocks=9,
        limit=16,
    )(*wanted, own, z1, z2, f1, f2, f3, peak, over, rd, one)
    two, one = along_z(two, -2, peers), along_z(one, -1, peers)
    (mine,) = call(add_two_kernel, (array(block, F32),), [VM] * 2, limit=4)(mine, two)
    key_grad, value_grad = call(final_kernel, (array((T, D), F32),) * 2, [VM] * 2, limit=4)(mine, one)
    return attended, query_grad, key_grad, value_grad


def solution(mesh):
    tokens = P("peer", "head")
    return jax.shard_map(
        body,
        mesh=mesh,
        in_specs=(tokens, tokens, tokens, tokens, P()),
        out_specs=(tokens, tokens, tokens, tokens),
        check_vma=False,
    )
```

```python
import functools
import math

import jax
import jax.numpy as jnp
from jax import lax
from jax.experimental import pallas as pl
from jax.experimental.pallas import tpu as pltpu
from jax.sharding import PartitionSpec as P

T = 256
D = 128
H = 4
ROW = 4
F32 = jnp.float32
BF16 = jnp.bfloat16
NEG = -1e30
SCALE = D**-0.5
TO_EXP2 = SCALE * math.log2(math.e)
LONG = (((1,), (1,)), ((), ()))
PLAIN = (((1,), (0,)), ((), ()))
VM = pl.BlockSpec(memory_space=pltpu.VMEM)
ANY = pl.BlockSpec(memory_space=pl.ANY)
SM = pl.BlockSpec(memory_space=pltpu.SMEM)


def dot(a, b, dims):
    return lax.dot_general(a, b, dims, preferred_element_type=F32)


def head(ref, h):
    return ref[:, h * D : (h + 1) * D]


def doc_starts(lengths_ref, first):
    place = first + lax.broadcasted_iota(jnp.int32, (1, T), 1)
    start = jnp.int32(0)
    own = jnp.zeros((1, T), jnp.int32)
    for i in range(lengths_ref.shape[0]):
        own = jnp.where(place >= start, start, own)
        start = start + lengths_ref[i]
    return own


def scores(q_ref, g_ref, key, value, hidden, index, m_ref, t_ref, r_ref, p_ref=None, dp_ref=None):
    for h in range(H):
        s = dot(key, head(q_ref, h), LONG)
        dp = dot(value, head(g_ref, h), LONG)
        s = jnp.where(hidden, NEG, s)
        m = jnp.max(s, axis=0, keepdims=True)
        p = jnp.exp2((s - m) * TO_EXP2)
        if p_ref is not None:
            p_ref[index, h] = p
            dp_ref[index, h] = dp
        m_ref[index, h : h + 1] = m
        t_ref[index, h : h + 1] = jnp.sum(p, axis=0, keepdims=True)
        r_ref[index, h : h + 1] = jnp.sum(p * dp, axis=0, keepdims=True)


def pair_kernel(k_ref, v_ref, out_ref):
    out_ref[0] = k_ref[...]
    out_ref[1] = v_ref[...]


def hold_kernel(lengths_ref, q_ref, g_ref, q_out, g_out, starts_ref):
    q_out[...] = q_ref[...]
    g_out[...] = g_ref[...]
    starts_ref[...] = doc_starts(lengths_ref, lax.axis_index("peer") * T)


def pack_kernel(_, own_ref, z1_ref, z2_ref, *out_refs):
    x = lax.rem(lax.axis_index("peer"), ROW)
    for d, ref in enumerate(out_refs, 1):

        @pl.when(x + d < ROW)
        def _(ref=ref):
            ref[0] = own_ref[...]

        @pl.when(x + d >= ROW)
        def _(ref=ref):
            ref[0] = z2_ref[...]

        ref[1] = z1_ref[...]


def near_hidden(first, starts, block):
    rows = lax.broadcasted_iota(jnp.int32, (T, 1), 0)
    hidden = (rows + (first - block * ROW * T)) < starts
    if block == 0:
        hidden = hidden | (rows > lax.broadcasted_iota(jnp.int32, (1, T), 1))
    return hidden


def far_hidden(first, starts, behind):
    rows = lax.broadcasted_iota(jnp.int32, (T, 1), 0)
    return (rows + (first - behind * T)) < starts


def near_kernel(starts_ref, q_ref, g_ref, own_ref, z1_ref, z2_ref, m_ref, t_ref, r_ref):
    first = lax.axis_index("peer") * T
    starts = starts_ref[...]
    for i, ref in enumerate((own_ref, z1_ref, z2_ref)):
        scores(q_ref, g_ref, ref[0], ref[1], near_hidden(first, starts, i), i, m_ref, t_ref, r_ref)


def behind(d, kind, x):
    return jnp.where((x >= d) ^ (kind == 1), d, ROW + d)


def key_side(q_ref, g_ref, pb_ref, ds_ref):
    dk = sum(dot(ds_ref[h], head(q_ref, h), PLAIN) for h in range(H))
    dv = sum(dot(pb_ref[h], head(g_ref, h), PLAIN) for h in range(H))
    return dk * SCALE, dv


def far_scores(d, starts_ref, q_ref, g_ref, far_ref, p_ref, dp_ref, m_ref, t_ref, r_ref):
    peer = lax.axis_index("peer")
    first = peer * T
    starts = starts_ref[...]
    for i in range(2):
        hidden = far_hidden(first, starts, behind(d, i, lax.rem(peer, ROW)))
        scores(q_ref, g_ref, far_ref[i, 0], far_ref[i, 1], hidden, i, m_ref, t_ref, r_ref, p_ref, dp_ref)


def far_back(p_ref, dp_ref, w_ref, rd_ref, q_ref, g_ref, back_ref, pb_ref, ds_ref):
    for i in range(2):
        for h in range(H):
            pn = p_ref[i, h] * w_ref[i, h : h + 1]
            pb_ref[i, h] = pn.astype(BF16)
            ds_ref[i, h] = (pn * (dp_ref[i, h] - rd_ref[h : h + 1])).astype(BF16)
        dk, dv = key_side(q_ref, g_ref, pb_ref.at[i], ds_ref.at[i])
        back_ref[i, 0] = dk.astype(BF16)
        back_ref[i, 1] = dv.astype(BF16)


def last_kernel(
    starts_ref, q_ref, g_ref, far_ref, mn, tn, rn, m1, t1, r1, p2_ref, dp2_ref, m2, t2, r2,
    b2_ref, peak_ref, over_ref, rd_ref, w1_ref, w3_ref, p3_ref, dp3_ref,
    m_ref, t_ref, r_ref, w2_ref, pb_ref, ds_ref,
):
    far_scores(3, starts_ref, q_ref, g_ref, far_ref, p3_ref, dp3_ref, m_ref, t_ref, r_ref)

    def each(near, *pairs):
        return [near[b] for b in range(3)] + [ref[b] for ref in pairs for b in range(2)]

    peaks, totals, dots = each(mn, m1, m2, m_ref), each(tn, t1, t2, t_ref), each(rn, r1, r2, r_ref)
    peak = functools.reduce(jnp.maximum, peaks)
    factors = [jnp.exp2((m - peak) * TO_EXP2) for m in peaks]
    over = 1.0 / sum(f * t for f, t in zip(factors, totals))
    peak_ref[...] = peak
    over_ref[...] = over
    rd_ref[...] = sum(f * r for f, r in zip(factors, dots)) * over
    for n, ref in enumerate((w1_ref, w2_ref, w3_ref)):
        for b in range(2):
            ref[b] = factors[3 + 2 * n + b] * over
    far_back(p2_ref, dp2_ref, w2_ref, rd_ref, q_ref, g_ref, b2_ref, pb_ref, ds_ref)


def sides_kernel(q_ref, g_ref, rd_ref, p1_ref, dp1_ref, w1_ref, p3_ref, dp3_ref, w3_ref, b1_ref, b3_ref, pb_ref, ds_ref):
    far_back(p1_ref, dp1_ref, w1_ref, rd_ref, q_ref, g_ref, b1_ref, pb_ref, ds_ref)
    far_back(p3_ref, dp3_ref, w3_ref, rd_ref, q_ref, g_ref, b3_ref, pb_ref, ds_ref)


def rest_kernel(
    starts_ref, q_ref, g_ref, own_ref, z1_ref, z2_ref, f1_ref, f2_ref, f3_ref, peak_ref, over_ref, rd_ref,
    out_ref, dq_ref, near_ref, o_acc, dq_acc, pb_ref, ds_ref,
):
    peer = lax.axis_index("peer")
    x = lax.rem(peer, ROW)
    first = peer * T
    starts = starts_ref[...]
    near = (own_ref, z1_ref, z2_ref)
    for b in range(9):
        if b < 3:
            key, value = near[b][0], near[b][1]
            hidden = near_hidden(first, starts, b)
        else:
            d, kind = (b - 3) // 2 + 1, (b - 3) % 2
            ref = (f1_ref, f2_ref, f3_ref)[d - 1]
            key, value = ref[kind, 0], ref[kind, 1]
            hidden = far_hidden(first, starts, behind(d, kind, x))
        pb, ds = pb_ref.at[b % 2], ds_ref.at[b % 2]
        for h in range(H):
            s = dot(key, head(q_ref, h), LONG)
            dp = dot(value, head(g_ref, h), LONG)
            s = jnp.where(hidden, NEG, s)
            pn = jnp.exp2((s - peak_ref[h : h + 1]) * TO_EXP2) * over_ref[h : h + 1]
            pb[h] = pn.astype(BF16)
            ds[h] = (pn * (dp - rd_ref[h : h + 1])).astype(BF16)
        kt, vt = key.T, value.T
        for h in range(H):
            o, dq = dot(vt, pb[h], PLAIN), dot(kt, ds[h], PLAIN)
            o_acc[h] = o if b == 0 else o_acc[h] + o
            dq_acc[h] = dq if b == 0 else dq_acc[h] + dq
        if b < 3:
            near_ref[b, 0], near_ref[b, 1] = key_side(q_ref, g_ref, pb, ds)

    for h in range(H):
        out_ref[:, h * D : (h + 1) * D] = o_acc[h].T.astype(BF16)
        dq_ref[:, h * D : (h + 1) * D] = dq_acc[h].T * SCALE


def add_back(d, ref, own, one, two):
    same = lax.rem(lax.axis_index("peer"), ROW) + d < ROW
    a, b = ref[0].astype(F32), ref[1].astype(F32)
    return own + jnp.where(same, a, 0.0), one + b, two + jnp.where(same, 0.0, a)


def gather_first_kernel(mine_ref, r2_ref, out_ref):
    for i, total in enumerate(add_back(2, r2_ref, mine_ref[0], mine_ref[1], mine_ref[2])):
        out_ref[i] = total


def gather_one_kernel(mine_ref, r1_ref, out_ref):
    for i, total in enumerate(add_back(1, r1_ref, mine_ref[0], mine_ref[1], mine_ref[2])):
        out_ref[i] = total


def gather_kernel(mine_ref, r3_ref, own_ref, one_ref, two_ref):
    own, one, two = add_back(3, r3_ref, mine_ref[0], mine_ref[1], mine_ref[2])
    own_ref[...] = own
    one_ref[...] = one.astype(BF16)
    two_ref[...] = two.astype(BF16)


def add_two_kernel(own_ref, two_ref, out_ref):
    out_ref[...] = own_ref[...] + two_ref[...].astype(F32)


def final_kernel(own_ref, one_ref, dk_ref, dv_ref):
    dk_ref[...] = own_ref[0] + one_ref[0].astype(F32)
    dv_ref[...] = own_ref[1] + one_ref[1].astype(F32)


def along_z(block, rows, peers):
    far = rows * ROW
    return lax.ppermute(block, "peer", [(i, i + far) for i in range(peers) if 0 <= i + far < peers])


def along_x(block, columns, peers):
    return lax.ppermute(block, "peer", [(i, i - i % ROW + (i + columns) % ROW) for i in range(peers)])


def call(kernel, out, specs, scratch=(), blocks=0, limit=24, first=VM):
    return pl.pallas_call(
        kernel,
        out_shape=out,
        in_specs=specs,
        out_specs=(first,) + tuple(VM for _ in out[1:]),
        scratch_shapes=list(scratch),
        compiler_params=pltpu.CompilerParams(vmem_limit_bytes=limit << 20),
        cost_estimate=pl.CostEstimate(
            flops=blocks * H * T * T * D * 4, bytes_accessed=1 << 20, transcendentals=blocks * H * T * T
        ),
    )


def body(queries, keys, values, grad_out, doc_lengths):
    peers = lax.axis_size("peer")
    array = jax.ShapeDtypeStruct
    block, stats = (2, T, D), (H, T)
    pair = array((2, *block), BF16)
    tiles, sums = (array((2, H, T, T), F32),) * 2, (array((2, *stats), F32),) * 3
    staged = [pltpu.VMEM((2, H, T, T), BF16)] * 2
    (own,) = call(pair_kernel, (array(block, BF16),), [VM] * 2, limit=4)(keys, values)
    z1 = along_z(own, 1, peers)
    z2 = along_z(own, 2, peers)
    queries, grad_out, starts = call(
        hold_kernel,
        (array((T, H * D), BF16), array((T, H * D), BF16), array((1, T), jnp.int32)),
        [SM] + [VM] * 2,
        blocks=1,
        limit=4,
    )(doc_lengths, queries, grad_out)
    wanted = (starts, queries, grad_out)
    packed = call(pack_kernel, (pair,) * 3, [VM] * 4, limit=4)(starts, own, z1, z2)
    f1, f2, f3 = (along_x(p, d, peers) for d, p in enumerate(packed, 1))
    near = call(near_kernel, (array((3, *stats), F32),) * 3, [VM] * 6, blocks=3, limit=8)(*wanted, own, z1, z2)
    arrive = {d: call(functools.partial(far_scores, d), tiles + sums, [VM] * 4, blocks=2, limit=8) for d in (1, 2)}
    p2, dp2, *sums2 = arrive[2](*wanted, f2)
    p1, dp1, *sums1 = arrive[1](*wanted, f1)
    b2, peak, over, rd, w1, w3, p3, dp3 = call(
        last_kernel,
        (pair,) + (array(stats, F32),) * 3 + (array((2, *stats), F32),) * 2 + tiles,
        [VM] * 15,
        [pltpu.VMEM((2, *stats), F32)] * 4 + staged,
        blocks=4,
        limit=8,
    )(*wanted, f3, *near, *sums1, p2, dp2, *sums2)
    r2 = along_x(b2, -2, peers)
    b1, b3 = call(sides_kernel, (pair,) * 2, [VM] * 9, staged, blocks=4, limit=8)(
        queries, grad_out, rd, p1, dp1, w1, p3, dp3, w3
    )
    r1, r3 = along_x(b1, -1, peers), along_x(b3, -3, peers)
    attended, query_grad, mine = call(
        rest_kernel,
        (array((T, H * D), BF16), array((T, H * D), F32), array((3, *block), F32)),
        [VM] * 12,
        [pltpu.VMEM((H, D, T), F32)] * 2 + staged,
        blocks=9,
        limit=16,
    )(*wanted, own, z1, z2, f1, f2, f3, peak, over, rd)
    (mine,) = call(gather_first_kernel, (array((3, *block), F32),), [VM] * 2, limit=4)(mine, r2)
    (mine,) = call(gather_one_kernel, (array((3, *block), F32),), [VM] * 2, limit=4)(mine, r1)
    mine, one, two = call(
        gather_kernel, (array(block, F32), array(block, BF16), array(block, BF16)), [VM] * 2, limit=4
    )(mine, r3)
    two, one = along_z(two, -2, peers), along_z(one, -1, peers)
    (mine,) = call(add_two_kernel, (array(block, F32),), [VM] * 2, limit=4)(mine, two)
    key_grad, value_grad = call(final_kernel, (array((T, D), F32),) * 2, [VM] * 2, limit=4)(mine, one)
    return attended, query_grad, key_grad, value_grad


def solution(mesh):
    tokens = P("peer", "head")
    return jax.shard_map(
        body,
        mesh=mesh,
        in_specs=(tokens, tokens, tokens, tokens, P()),
        out_specs=(tokens, tokens, tokens, tokens),
        check_vma=False,
    )
```

```python
import functools
import math

import jax
import jax.numpy as jnp
from jax import lax
from jax.experimental import pallas as pl
from jax.experimental.pallas import tpu as pltpu
from jax.sharding import PartitionSpec as P

T = 256
D = 128
H = 4
ROW = 4
F32 = jnp.float32
BF16 = jnp.bfloat16
NEG = -1e30
SCALE = D**-0.5
TO_EXP2 = SCALE * math.log2(math.e)
LONG = (((1,), (1,)), ((), ()))
PLAIN = (((1,), (0,)), ((), ()))
VM = pl.BlockSpec(memory_space=pltpu.VMEM)
ANY = pl.BlockSpec(memory_space=pl.ANY)
SM = pl.BlockSpec(memory_space=pltpu.SMEM)


def dot(a, b, dims):
    return lax.dot_general(a, b, dims, preferred_element_type=F32)


def head(ref, h):
    return ref[:, h * D : (h + 1) * D]


def doc_starts(lengths_ref, first):
    place = first + lax.broadcasted_iota(jnp.int32, (1, T), 1)
    start = jnp.int32(0)
    own = jnp.zeros((1, T), jnp.int32)
    for i in range(lengths_ref.shape[0]):
        own = jnp.where(place >= start, start, own)
        start = start + lengths_ref[i]
    return own


def scores(q_ref, g_ref, key, value, hidden, index, m_ref, t_ref, r_ref, p_ref=None, dp_ref=None):
    for h in range(H):
        s = dot(key, head(q_ref, h), LONG)
        dp = dot(value, head(g_ref, h), LONG)
        s = jnp.where(hidden, NEG, s)
        m = jnp.max(s, axis=0, keepdims=True)
        p = jnp.exp2((s - m) * TO_EXP2)
        if p_ref is not None:
            p_ref[index, h] = p
            dp_ref[index, h] = dp
        m_ref[index, h : h + 1] = m
        t_ref[index, h : h + 1] = jnp.sum(p, axis=0, keepdims=True)
        r_ref[index, h : h + 1] = jnp.sum(p * dp, axis=0, keepdims=True)


def pair_kernel(k_ref, v_ref, out_ref):
    out_ref[0] = k_ref[...]
    out_ref[1] = v_ref[...]


def hold_kernel(lengths_ref, q_ref, g_ref, q_out, g_out, starts_ref):
    q_out[...] = q_ref[...]
    g_out[...] = g_ref[...]
    starts_ref[...] = doc_starts(lengths_ref, lax.axis_index("peer") * T)


def pack_kernel(_, own_ref, z1_ref, z2_ref, *out_refs):
    x = lax.rem(lax.axis_index("peer"), ROW)
    for d, ref in enumerate(out_refs, 1):

        @pl.when(x + d < ROW)
        def _(ref=ref):
            ref[0] = own_ref[...]

        @pl.when(x + d >= ROW)
        def _(ref=ref):
            ref[0] = z2_ref[...]

        ref[1] = z1_ref[...]


def near_hidden(first, starts, block):
    rows = lax.broadcasted_iota(jnp.int32, (T, 1), 0)
    hidden = (rows + (first - block * ROW * T)) < starts
    if block == 0:
        hidden = hidden | (rows > lax.broadcasted_iota(jnp.int32, (1, T), 1))
    return hidden


def far_hidden(first, starts, behind):
    rows = lax.broadcasted_iota(jnp.int32, (T, 1), 0)
    return (rows + (first - behind * T)) < starts


def near_kernel(starts_ref, q_ref, g_ref, own_ref, z1_ref, z2_ref, m_ref, t_ref, r_ref):
    first = lax.axis_index("peer") * T
    starts = starts_ref[...]
    for i, ref in enumerate((own_ref, z1_ref, z2_ref)):
        scores(q_ref, g_ref, ref[0], ref[1], near_hidden(first, starts, i), i, m_ref, t_ref, r_ref)


def behind(d, kind, x):
    return jnp.where((x >= d) ^ (kind == 1), d, ROW + d)


def key_side(q_ref, g_ref, pb_ref, ds_ref):
    dk = sum(dot(ds_ref[h], head(q_ref, h), PLAIN) for h in range(H))
    dv = sum(dot(pb_ref[h], head(g_ref, h), PLAIN) for h in range(H))
    return dk * SCALE, dv


def far_scores(d, starts_ref, q_ref, g_ref, far_ref, p_ref, dp_ref, m_ref, t_ref, r_ref):
    peer = lax.axis_index("peer")
    first = peer * T
    starts = starts_ref[...]
    for i in range(2):
        hidden = far_hidden(first, starts, behind(d, i, lax.rem(peer, ROW)))
        scores(q_ref, g_ref, far_ref[i, 0], far_ref[i, 1], hidden, i, m_ref, t_ref, r_ref, p_ref, dp_ref)


def far_back(p_ref, dp_ref, w_ref, rd_ref, q_ref, g_ref, back_ref, pb_ref, ds_ref):
    for i in range(2):
        for h in range(H):
            pn = p_ref[i, h] * w_ref[i, h : h + 1]
            pb_ref[i, h] = pn.astype(BF16)
            ds_ref[i, h] = (pn * (dp_ref[i, h] - rd_ref[h : h + 1])).astype(BF16)
        dk, dv = key_side(q_ref, g_ref, pb_ref.at[i], ds_ref.at[i])
        back_ref[i, 0] = dk.astype(BF16)
        back_ref[i, 1] = dv.astype(BF16)


def last_kernel(
    starts_ref, q_ref, g_ref, far_ref, mn, tn, rn, m1, t1, r1, p2_ref, dp2_ref, m2, t2, r2,
    b2_ref, peak_ref, over_ref, rd_ref, w1_ref, w3_ref, p3_ref, dp3_ref,
    m_ref, t_ref, r_ref, w2_ref, pb_ref, ds_ref,
):
    far_scores(3, starts_ref, q_ref, g_ref, far_ref, p3_ref, dp3_ref, m_ref, t_ref, r_ref)

    def each(near, *pairs):
        return [near[b] for b in range(3)] + [ref[b] for ref in pairs for b in range(2)]

    peaks, totals, dots = each(mn, m1, m2, m_ref), each(tn, t1, t2, t_ref), each(rn, r1, r2, r_ref)
    peak = functools.reduce(jnp.maximum, peaks)
    factors = [jnp.exp2((m - peak) * TO_EXP2) for m in peaks]
    over = 1.0 / sum(f * t for f, t in zip(factors, totals))
    peak_ref[...] = peak
    over_ref[...] = over
    rd_ref[...] = sum(f * r for f, r in zip(factors, dots)) * over
    for n, ref in enumerate((w1_ref, w2_ref, w3_ref)):
        for b in range(2):
            ref[b] = factors[3 + 2 * n + b] * over
    far_back(p2_ref, dp2_ref, w2_ref, rd_ref, q_ref, g_ref, b2_ref, pb_ref, ds_ref)


def sides_kernel(q_ref, g_ref, rd_ref, p1_ref, dp1_ref, w1_ref, p3_ref, dp3_ref, w3_ref, b1_ref, b3_ref, pb_ref, ds_ref):
    far_back(p1_ref, dp1_ref, w1_ref, rd_ref, q_ref, g_ref, b1_ref, pb_ref, ds_ref)
    far_back(p3_ref, dp3_ref, w3_ref, rd_ref, q_ref, g_ref, b3_ref, pb_ref, ds_ref)


def weights(q_ref, g_ref, key, value, hidden, peak_ref, over_ref, rd_ref, pb_ref, ds_ref):
    for h in range(H):
        s = dot(key, head(q_ref, h), LONG)
        dp = dot(value, head(g_ref, h), LONG)
        s = jnp.where(hidden, NEG, s)
        pn = jnp.exp2((s - peak_ref[h : h + 1]) * TO_EXP2) * over_ref[h : h + 1]
        pb_ref[h] = pn.astype(BF16)
        ds_ref[h] = (pn * (dp - rd_ref[h : h + 1])).astype(BF16)


def near_back_kernel(starts_ref, q_ref, g_ref, own_ref, z1_ref, z2_ref, peak_ref, over_ref, rd_ref, near_ref, pb_ref, ds_ref):
    first = lax.axis_index("peer") * T
    for b, ref in enumerate((own_ref, z1_ref, z2_ref)):
        pb, ds = pb_ref.at[b % 2], ds_ref.at[b % 2]
        hidden = near_hidden(first, starts_ref[...], b)
        weights(q_ref, g_ref, ref[0], ref[1], hidden, peak_ref, over_ref, rd_ref, pb, ds)
        near_ref[b, 0], near_ref[b, 1] = key_side(q_ref, g_ref, pb, ds)


def query_side_kernel(
    starts_ref, q_ref, g_ref, own_ref, z1_ref, z2_ref, f1_ref, f2_ref, f3_ref, peak_ref, over_ref, rd_ref, _,
    out_ref, dq_ref, o_acc, dq_acc, pb_ref, ds_ref,
):
    peer = lax.axis_index("peer")
    x = lax.rem(peer, ROW)
    first = peer * T
    starts = starts_ref[...]
    near = (own_ref, z1_ref, z2_ref)
    for b in range(9):
        if b < 3:
            key, value = near[b][0], near[b][1]
            hidden = near_hidden(first, starts, b)
        else:
            d, kind = (b - 3) // 2 + 1, (b - 3) % 2
            ref = (f1_ref, f2_ref, f3_ref)[d - 1]
            key, value = ref[kind, 0], ref[kind, 1]
            hidden = far_hidden(first, starts, behind(d, kind, x))
        pb, ds = pb_ref.at[b % 2], ds_ref.at[b % 2]
        weights(q_ref, g_ref, key, value, hidden, peak_ref, over_ref, rd_ref, pb, ds)
        kt, vt = key.T, value.T
        for h in range(H):
            o, dq = dot(vt, pb[h], PLAIN), dot(kt, ds[h], PLAIN)
            o_acc[h] = o if b == 0 else o_acc[h] + o
            dq_acc[h] = dq if b == 0 else dq_acc[h] + dq

    for h in range(H):
        out_ref[:, h * D : (h + 1) * D] = o_acc[h].T.astype(BF16)
        dq_ref[:, h * D : (h + 1) * D] = dq_acc[h].T * SCALE


def add_back(d, ref, own, one, two):
    same = lax.rem(lax.axis_index("peer"), ROW) + d < ROW
    a, b = ref[0].astype(F32), ref[1].astype(F32)
    return own + jnp.where(same, a, 0.0), one + b, two + jnp.where(same, 0.0, a)


def gather_first_kernel(mine_ref, r2_ref, out_ref):
    for i, total in enumerate(add_back(2, r2_ref, mine_ref[0], mine_ref[1], mine_ref[2])):
        out_ref[i] = total


def gather_one_kernel(mine_ref, r1_ref, out_ref):
    for i, total in enumerate(add_back(1, r1_ref, mine_ref[0], mine_ref[1], mine_ref[2])):
        out_ref[i] = total


def gather_kernel(mine_ref, r3_ref, own_ref, one_ref, two_ref):
    own, one, two = add_back(3, r3_ref, mine_ref[0], mine_ref[1], mine_ref[2])
    own_ref[...] = own
    one_ref[...] = one.astype(BF16)
    two_ref[...] = two.astype(BF16)


def add_two_kernel(own_ref, two_ref, out_ref):
    out_ref[...] = own_ref[...] + two_ref[...].astype(F32)


def final_kernel(own_ref, one_ref, dk_ref, dv_ref):
    dk_ref[...] = own_ref[0] + one_ref[0].astype(F32)
    dv_ref[...] = own_ref[1] + one_ref[1].astype(F32)


def along_z(block, rows, peers):
    far = rows * ROW
    return lax.ppermute(block, "peer", [(i, i + far) for i in range(peers) if 0 <= i + far < peers])


def along_x(block, columns, peers):
    return lax.ppermute(block, "peer", [(i, i - i % ROW + (i + columns) % ROW) for i in range(peers)])


def call(kernel, out, specs, scratch=(), blocks=0, limit=24, first=VM):
    return pl.pallas_call(
        kernel,
        out_shape=out,
        in_specs=specs,
        out_specs=(first,) + tuple(VM for _ in out[1:]),
        scratch_shapes=list(scratch),
        compiler_params=pltpu.CompilerParams(vmem_limit_bytes=limit << 20),
        cost_estimate=pl.CostEstimate(
            flops=blocks * H * T * T * D * 4, bytes_accessed=1 << 20, transcendentals=blocks * H * T * T
        ),
    )


def body(queries, keys, values, grad_out, doc_lengths):
    peers = lax.axis_size("peer")
    array = jax.ShapeDtypeStruct
    block, stats = (2, T, D), (H, T)
    pair = array((2, *block), BF16)
    tiles, sums = (array((2, H, T, T), F32),) * 2, (array((2, *stats), F32),) * 3
    staged = [pltpu.VMEM((2, H, T, T), BF16)] * 2
    (own,) = call(pair_kernel, (array(block, BF16),), [VM] * 2, limit=4)(keys, values)
    z1 = along_z(own, 1, peers)
    z2 = along_z(own, 2, peers)
    queries, grad_out, starts = call(
        hold_kernel,
        (array((T, H * D), BF16), array((T, H * D), BF16), array((1, T), jnp.int32)),
        [SM] + [VM] * 2,
        blocks=1,
        limit=4,
    )(doc_lengths, queries, grad_out)
    wanted = (starts, queries, grad_out)
    packed = call(pack_kernel, (pair,) * 3, [VM] * 4, limit=4)(starts, own, z1, z2)
    f1, f2, f3 = (along_x(p, d, peers) for d, p in enumerate(packed, 1))
    near = call(near_kernel, (array((3, *stats), F32),) * 3, [VM] * 6, blocks=3, limit=8)(*wanted, own, z1, z2)
    arrive = {d: call(functools.partial(far_scores, d), tiles + sums, [VM] * 4, blocks=2, limit=8) for d in (1, 2)}
    p2, dp2, *sums2 = arrive[2](*wanted, f2)
    p1, dp1, *sums1 = arrive[1](*wanted, f1)
    b2, peak, over, rd, w1, w3, p3, dp3 = call(
        last_kernel,
        (pair,) + (array(stats, F32),) * 3 + (array((2, *stats), F32),) * 2 + tiles,
        [VM] * 15,
        [pltpu.VMEM((2, *stats), F32)] * 4 + staged,
        blocks=4,
        limit=8,
    )(*wanted, f3, *near, *sums1, p2, dp2, *sums2)
    r2 = along_x(b2, -2, peers)
    b1, b3 = call(sides_kernel, (pair,) * 2, [VM] * 9, staged, blocks=4, limit=8)(
        queries, grad_out, rd, p1, dp1, w1, p3, dp3, w3
    )
    r1, r3 = along_x(b1, -1, peers), along_x(b3, -3, peers)
    (mine,) = call(near_back_kernel, (array((3, *block), F32),), [VM] * 9, staged, blocks=3, limit=8)(
        *wanted, own, z1, z2, peak, over, rd
    )
    (mine,) = call(gather_first_kernel, (array((3, *block), F32),), [VM] * 2, limit=4)(mine, r2)
    (mine,) = call(gather_one_kernel, (array((3, *block), F32),), [VM] * 2, limit=4)(mine, r1)
    mine, one, two = call(
        gather_kernel, (array(block, F32), array(block, BF16), array(block, BF16)), [VM] * 2, limit=4
    )(mine, r3)
    attended, query_grad = call(
        query_side_kernel,
        (array((T, H * D), BF16), array((T, H * D), F32)),
        [VM] * 13,
        [pltpu.VMEM((H, D, T), F32)] * 2 + staged,
        blocks=9,
        limit=16,
    )(*wanted, own, z1, z2, f1, f2, f3, peak, over, rd, one)
    two, one = along_z(two, -2, peers), along_z(one, -1, peers)
    (mine,) = call(add_two_kernel, (array(block, F32),), [VM] * 2, limit=4)(mine, two)
    key_grad, value_grad = call(final_kernel, (array((T, D), F32),) * 2, [VM] * 2, limit=4)(mine, one)
    return attended, query_grad, key_grad, value_grad


def solution(mesh):
    tokens = P("peer", "head")
    return jax.shard_map(
        body,
        mesh=mesh,
        in_specs=(tokens, tokens, tokens, tokens, P()),
        out_specs=(tokens, tokens, tokens, tokens),
        check_vma=False,
    )
```

```python
import functools
import math

import jax
import jax.numpy as jnp
from jax import lax
from jax.experimental import pallas as pl
from jax.experimental.pallas import tpu as pltpu
from jax.sharding import PartitionSpec as P

T = 256
D = 128
H = 4
ROW = 4
F32 = jnp.float32
BF16 = jnp.bfloat16
NEG = -1e30
SCALE = D**-0.5
TO_EXP2 = SCALE * math.log2(math.e)
LONG = (((1,), (1,)), ((), ()))
PLAIN = (((1,), (0,)), ((), ()))
VM = pl.BlockSpec(memory_space=pltpu.VMEM)
ANY = pl.BlockSpec(memory_space=pl.ANY)
SM = pl.BlockSpec(memory_space=pltpu.SMEM)


def dot(a, b, dims):
    return lax.dot_general(a, b, dims, preferred_element_type=F32)


def head(ref, h):
    return ref[:, h * D : (h + 1) * D]


def doc_starts(lengths_ref, first):
    place = first + lax.broadcasted_iota(jnp.int32, (1, T), 1)
    start = jnp.int32(0)
    own = jnp.zeros((1, T), jnp.int32)
    for i in range(lengths_ref.shape[0]):
        own = jnp.where(place >= start, start, own)
        start = start + lengths_ref[i]
    return own


def scores(q_ref, g_ref, key, value, hidden, index, m_ref, t_ref, r_ref, p_ref=None, dp_ref=None):
    for h in range(H):
        s = dot(key, head(q_ref, h), LONG)
        dp = dot(value, head(g_ref, h), LONG)
        s = jnp.where(hidden, NEG, s)
        m = jnp.max(s, axis=0, keepdims=True)
        p = jnp.exp2((s - m) * TO_EXP2)
        if p_ref is not None:
            p_ref[index, h] = p
            dp_ref[index, h] = dp
        m_ref[index, h : h + 1] = m
        t_ref[index, h : h + 1] = jnp.sum(p, axis=0, keepdims=True)
        r_ref[index, h : h + 1] = jnp.sum(p * dp, axis=0, keepdims=True)


def pair_kernel(k_ref, v_ref, out_ref, sem):
    copies = [pltpu.make_async_copy(r, out_ref.at[i], sem.at[i]) for i, r in enumerate((k_ref, v_ref))]
    for copy in copies:
        copy.start()
    for copy in copies:
        copy.wait()


def hold_kernel(lengths_ref, q_ref, g_ref, q_out, g_out, starts_ref):
    q_out[...] = q_ref[...]
    g_out[...] = g_ref[...]
    starts_ref[...] = doc_starts(lengths_ref, lax.axis_index("peer") * T)


def pack_kernel(_, own_ref, z1_ref, z2_ref, *out_refs):
    x = lax.rem(lax.axis_index("peer"), ROW)
    for d, ref in enumerate(out_refs, 1):

        @pl.when(x + d < ROW)
        def _(ref=ref):
            ref[0] = own_ref[...]

        @pl.when(x + d >= ROW)
        def _(ref=ref):
            ref[0] = z2_ref[...]

        ref[1] = z1_ref[...]


def near_hidden(first, starts, block):
    rows = lax.broadcasted_iota(jnp.int32, (T, 1), 0)
    hidden = (rows + (first - block * ROW * T)) < starts
    if block == 0:
        hidden = hidden | (rows > lax.broadcasted_iota(jnp.int32, (1, T), 1))
    return hidden


def far_hidden(first, starts, behind):
    rows = lax.broadcasted_iota(jnp.int32, (T, 1), 0)
    return (rows + (first - behind * T)) < starts


def near_kernel(starts_ref, q_ref, g_ref, own_ref, z1_ref, z2_ref, m_ref, t_ref, r_ref):
    first = lax.axis_index("peer") * T
    starts = starts_ref[...]
    for i, ref in enumerate((own_ref, z1_ref, z2_ref)):
        scores(q_ref, g_ref, ref[0], ref[1], near_hidden(first, starts, i), i, m_ref, t_ref, r_ref)


def behind(d, kind, x):
    return jnp.where((x >= d) ^ (kind == 1), d, ROW + d)


def key_side(q_ref, g_ref, pb_ref, ds_ref):
    dk = sum(dot(ds_ref[h], head(q_ref, h), PLAIN) for h in range(H))
    dv = sum(dot(pb_ref[h], head(g_ref, h), PLAIN) for h in range(H))
    return dk * SCALE, dv


def far_scores(d, starts_ref, q_ref, g_ref, far_ref, p_ref, dp_ref, m_ref, t_ref, r_ref):
    peer = lax.axis_index("peer")
    first = peer * T
    starts = starts_ref[...]
    for i in range(2):
        hidden = far_hidden(first, starts, behind(d, i, lax.rem(peer, ROW)))
        scores(q_ref, g_ref, far_ref[i, 0], far_ref[i, 1], hidden, i, m_ref, t_ref, r_ref, p_ref, dp_ref)


def far_back(p_ref, dp_ref, w_ref, rd_ref, q_ref, g_ref, back_ref, pb_ref, ds_ref):
    for i in range(2):
        for h in range(H):
            pn = p_ref[i, h] * w_ref[i, h : h + 1]
            pb_ref[i, h] = pn.astype(BF16)
            ds_ref[i, h] = (pn * (dp_ref[i, h] - rd_ref[h : h + 1])).astype(BF16)
        dk, dv = key_side(q_ref, g_ref, pb_ref.at[i], ds_ref.at[i])
        back_ref[i, 0] = dk.astype(BF16)
        back_ref[i, 1] = dv.astype(BF16)


def last_kernel(
    starts_ref, q_ref, g_ref, far_ref, mn, tn, rn, m1, t1, r1, p2_ref, dp2_ref, m2, t2, r2,
    b2_ref, peak_ref, over_ref, rd_ref, w1_ref, w3_ref, p3_ref, dp3_ref,
    m_ref, t_ref, r_ref, w2_ref, pb_ref, ds_ref,
):
    far_scores(3, starts_ref, q_ref, g_ref, far_ref, p3_ref, dp3_ref, m_ref, t_ref, r_ref)

    def each(near, *pairs):
        return [near[b] for b in range(3)] + [ref[b] for ref in pairs for b in range(2)]

    peaks, totals, dots = each(mn, m1, m2, m_ref), each(tn, t1, t2, t_ref), each(rn, r1, r2, r_ref)
    peak = functools.reduce(jnp.maximum, peaks)
    factors = [jnp.exp2((m - peak) * TO_EXP2) for m in peaks]
    over = 1.0 / sum(f * t for f, t in zip(factors, totals))
    peak_ref[...] = peak
    over_ref[...] = over
    rd_ref[...] = sum(f * r for f, r in zip(factors, dots)) * over
    for n, ref in enumerate((w1_ref, w2_ref, w3_ref)):
        for b in range(2):
            ref[b] = factors[3 + 2 * n + b] * over
    far_back(p2_ref, dp2_ref, w2_ref, rd_ref, q_ref, g_ref, b2_ref, pb_ref, ds_ref)


def sides_kernel(q_ref, g_ref, rd_ref, p1_ref, dp1_ref, w1_ref, p3_ref, dp3_ref, w3_ref, b1_ref, b3_ref, pb_ref, ds_ref):
    far_back(p1_ref, dp1_ref, w1_ref, rd_ref, q_ref, g_ref, b1_ref, pb_ref, ds_ref)
    far_back(p3_ref, dp3_ref, w3_ref, rd_ref, q_ref, g_ref, b3_ref, pb_ref, ds_ref)


def weights(q_ref, g_ref, key, value, hidden, peak_ref, over_ref, rd_ref, pb_ref, ds_ref):
    for h in range(H):
        s = dot(key, head(q_ref, h), LONG)
        dp = dot(value, head(g_ref, h), LONG)
        s = jnp.where(hidden, NEG, s)
        pn = jnp.exp2((s - peak_ref[h : h + 1]) * TO_EXP2) * over_ref[h : h + 1]
        pb_ref[h] = pn.astype(BF16)
        ds_ref[h] = (pn * (dp - rd_ref[h : h + 1])).astype(BF16)


def near_back_kernel(starts_ref, q_ref, g_ref, own_ref, z1_ref, z2_ref, peak_ref, over_ref, rd_ref, near_ref, pb_ref, ds_ref):
    first = lax.axis_index("peer") * T
    for b, ref in enumerate((own_ref, z1_ref, z2_ref)):
        pb, ds = pb_ref.at[b % 2], ds_ref.at[b % 2]
        hidden = near_hidden(first, starts_ref[...], b)
        weights(q_ref, g_ref, ref[0], ref[1], hidden, peak_ref, over_ref, rd_ref, pb, ds)
        near_ref[b, 0], near_ref[b, 1] = key_side(q_ref, g_ref, pb, ds)


def query_side_kernel(
    starts_ref, q_ref, g_ref, own_ref, z1_ref, z2_ref, f1_ref, f2_ref, f3_ref, peak_ref, over_ref, rd_ref, _,
    out_ref, dq_ref, o_acc, dq_acc, pb_ref, ds_ref,
):
    peer = lax.axis_index("peer")
    x = lax.rem(peer, ROW)
    first = peer * T
    starts = starts_ref[...]
    near = (own_ref, z1_ref, z2_ref)
    for b in range(9):
        if b < 3:
            key, value = near[b][0], near[b][1]
            hidden = near_hidden(first, starts, b)
        else:
            d, kind = (b - 3) // 2 + 1, (b - 3) % 2
            ref = (f1_ref, f2_ref, f3_ref)[d - 1]
            key, value = ref[kind, 0], ref[kind, 1]
            hidden = far_hidden(first, starts, behind(d, kind, x))
        pb, ds = pb_ref.at[b % 2], ds_ref.at[b % 2]
        weights(q_ref, g_ref, key, value, hidden, peak_ref, over_ref, rd_ref, pb, ds)
        kt, vt = key.T, value.T
        for h in range(H):
            o, dq = dot(vt, pb[h], PLAIN), dot(kt, ds[h], PLAIN)
            o_acc[h] = o if b == 0 else o_acc[h] + o
            dq_acc[h] = dq if b == 0 else dq_acc[h] + dq

    for h in range(H):
        out_ref[:, h * D : (h + 1) * D] = o_acc[h].T.astype(BF16)
        dq_ref[:, h * D : (h + 1) * D] = dq_acc[h].T * SCALE


def add_back(d, ref, own, one, two):
    same = lax.rem(lax.axis_index("peer"), ROW) + d < ROW
    a, b = ref[0].astype(F32), ref[1].astype(F32)
    return own + jnp.where(same, a, 0.0), one + b, two + jnp.where(same, 0.0, a)


def gather_first_kernel(mine_ref, r2_ref, out_ref):
    for i, total in enumerate(add_back(2, r2_ref, mine_ref[0], mine_ref[1], mine_ref[2])):
        out_ref[i] = total


def gather_one_kernel(mine_ref, r1_ref, out_ref):
    for i, total in enumerate(add_back(1, r1_ref, mine_ref[0], mine_ref[1], mine_ref[2])):
        out_ref[i] = total


def gather_kernel(mine_ref, r3_ref, own_ref, one_ref, two_ref):
    own, one, two = add_back(3, r3_ref, mine_ref[0], mine_ref[1], mine_ref[2])
    own_ref[...] = own
    one_ref[...] = one.astype(BF16)
    two_ref[...] = two.astype(BF16)


def add_two_kernel(own_ref, two_ref, out_ref):
    out_ref[...] = own_ref[...] + two_ref[...].astype(F32)


def final_kernel(own_ref, one_ref, dk_ref, dv_ref):
    dk_ref[...] = own_ref[0] + one_ref[0].astype(F32)
    dv_ref[...] = own_ref[1] + one_ref[1].astype(F32)


def along_z(block, rows, peers):
    far = rows * ROW
    return lax.ppermute(block, "peer", [(i, i + far) for i in range(peers) if 0 <= i + far < peers])


def along_x(block, columns, peers):
    return lax.ppermute(block, "peer", [(i, i - i % ROW + (i + columns) % ROW) for i in range(peers)])


def call(kernel, out, specs, scratch=(), blocks=0, limit=24, first=VM):
    return pl.pallas_call(
        kernel,
        out_shape=out,
        in_specs=specs,
        out_specs=(first,) + tuple(VM for _ in out[1:]),
        scratch_shapes=list(scratch),
        compiler_params=pltpu.CompilerParams(vmem_limit_bytes=limit << 20),
        cost_estimate=pl.CostEstimate(
            flops=blocks * H * T * T * D * 4, bytes_accessed=1 << 20, transcendentals=blocks * H * T * T
        ),
    )


def body(queries, keys, values, grad_out, doc_lengths):
    peers = lax.axis_size("peer")
    array = jax.ShapeDtypeStruct
    block, stats = (2, T, D), (H, T)
    pair = array((2, *block), BF16)
    tiles, sums = (array((2, H, T, T), F32),) * 2, (array((2, *stats), F32),) * 3
    staged = [pltpu.VMEM((2, H, T, T), BF16)] * 2
    (own,) = call(pair_kernel, (pltpu.VMEM(block, BF16),), [ANY] * 2, [pltpu.SemaphoreType.DMA((2,))], limit=54)(
        keys, values
    )
    z1 = along_z(own, 1, peers)
    z2 = along_z(own, 2, peers)
    queries, grad_out, starts = call(
        hold_kernel,
        (array((T, H * D), BF16), array((T, H * D), BF16), array((1, T), jnp.int32)),
        [SM] + [VM] * 2,
        blocks=1,
        limit=4,
    )(doc_lengths, queries, grad_out)
    wanted = (starts, queries, grad_out)
    packed = call(pack_kernel, (pair,) * 3, [VM] * 4, limit=4)(starts, own, z1, z2)
    f1, f2, f3 = (along_x(p, d, peers) for d, p in enumerate(packed, 1))
    near = call(near_kernel, (array((3, *stats), F32),) * 3, [VM] * 6, blocks=3, limit=8)(*wanted, own, z1, z2)
    arrive = {d: call(functools.partial(far_scores, d), tiles + sums, [VM] * 4, blocks=2, limit=8) for d in (1, 2)}
    p2, dp2, *sums2 = arrive[2](*wanted, f2)
    p1, dp1, *sums1 = arrive[1](*wanted, f1)
    b2, peak, over, rd, w1, w3, p3, dp3 = call(
        last_kernel,
        (pair,) + (array(stats, F32),) * 3 + (array((2, *stats), F32),) * 2 + tiles,
        [VM] * 15,
        [pltpu.VMEM((2, *stats), F32)] * 4 + staged,
        blocks=4,
        limit=8,
    )(*wanted, f3, *near, *sums1, p2, dp2, *sums2)
    r2 = along_x(b2, -2, peers)
    b1, b3 = call(sides_kernel, (pair,) * 2, [VM] * 9, staged, blocks=4, limit=8)(
        queries, grad_out, rd, p1, dp1, w1, p3, dp3, w3
    )
    r1, r3 = along_x(b1, -1, peers), along_x(b3, -3, peers)
    (mine,) = call(near_back_kernel, (array((3, *block), F32),), [VM] * 9, staged, blocks=3, limit=8)(
        *wanted, own, z1, z2, peak, over, rd
    )
    (mine,) = call(gather_first_kernel, (array((3, *block), F32),), [VM] * 2, limit=4)(mine, r2)
    (mine,) = call(gather_one_kernel, (array((3, *block), F32),), [VM] * 2, limit=4)(mine, r1)
    mine, one, two = call(
        gather_kernel, (array(block, F32), array(block, BF16), array(block, BF16)), [VM] * 2, limit=4
    )(mine, r3)
    attended, query_grad = call(
        query_side_kernel,
        (array((T, H * D), BF16), array((T, H * D), F32)),
        [VM] * 13,
        [pltpu.VMEM((H, D, T), F32)] * 2 + staged,
        blocks=9,
        limit=16,
    )(*wanted, own, z1, z2, f1, f2, f3, peak, over, rd, one)
    two, one = along_z(two, -2, peers), along_z(one, -1, peers)
    (mine,) = call(add_two_kernel, (array(block, F32),), [VM] * 2, limit=4)(mine, two)
    key_grad, value_grad = call(final_kernel, (array((T, D), F32),) * 2, [VM] * 2, limit=4)(mine, one)
    return attended, query_grad, key_grad, value_grad


def solution(mesh):
    tokens = P("peer", "head")
    return jax.shard_map(
        body,
        mesh=mesh,
        in_specs=(tokens, tokens, tokens, tokens, P()),
        out_specs=(tokens, tokens, tokens, tokens),
        check_vma=False,
    )
```

```python
import functools
import math

import jax
import jax.numpy as jnp
from jax import lax
from jax.experimental import pallas as pl
from jax.experimental.pallas import tpu as pltpu
from jax.sharding import PartitionSpec as P

T = 256
D = 128
H = 4
ROW = 4
F32 = jnp.float32
BF16 = jnp.bfloat16
NEG = -1e30
SCALE = D**-0.5
TO_EXP2 = SCALE * math.log2(math.e)
LONG = (((1,), (1,)), ((), ()))
PLAIN = (((1,), (0,)), ((), ()))
VM = pl.BlockSpec(memory_space=pltpu.VMEM)
ANY = pl.BlockSpec(memory_space=pl.ANY)
SM = pl.BlockSpec(memory_space=pltpu.SMEM)


def dot(a, b, dims):
    return lax.dot_general(a, b, dims, preferred_element_type=F32)


def head(ref, h):
    return ref[:, h * D : (h + 1) * D]


def doc_starts(lengths_ref, first):
    place = first + lax.broadcasted_iota(jnp.int32, (1, T), 1)
    start = jnp.int32(0)
    own = jnp.zeros((1, T), jnp.int32)
    for i in range(lengths_ref.shape[0]):
        own = jnp.where(place >= start, start, own)
        start = start + lengths_ref[i]
    return own


def scores(q_ref, g_ref, key, value, hidden, index, m_ref, t_ref, r_ref, p_ref=None, dp_ref=None):
    for h in range(H):
        s = dot(key, head(q_ref, h), LONG)
        dp = dot(value, head(g_ref, h), LONG)
        s = jnp.where(hidden, NEG, s)
        m = jnp.max(s, axis=0, keepdims=True)
        p = jnp.exp2((s - m) * TO_EXP2)
        if p_ref is not None:
            p_ref[index, h] = p
            dp_ref[index, h] = dp
        m_ref[index, h : h + 1] = m
        t_ref[index, h : h + 1] = jnp.sum(p, axis=0, keepdims=True)
        r_ref[index, h : h + 1] = jnp.sum(p * dp, axis=0, keepdims=True)


def pair_kernel(k_ref, v_ref, out_ref, sem):
    copies = [pltpu.make_async_copy(r, out_ref.at[i], sem.at[i]) for i, r in enumerate((k_ref, v_ref))]
    for copy in copies:
        copy.start()
    for copy in copies:
        copy.wait()


def hold_kernel(lengths_ref, q_ref, g_ref, q_out, g_out, starts_ref):
    q_out[...] = q_ref[...]
    g_out[...] = g_ref[...]
    starts_ref[...] = doc_starts(lengths_ref, lax.axis_index("peer") * T)


def pack_kernel(_, own_ref, z1_ref, z2_ref, *out_refs):
    x = lax.rem(lax.axis_index("peer"), ROW)
    for d, ref in enumerate(out_refs, 1):

        @pl.when(x + d < ROW)
        def _(ref=ref):
            ref[0] = own_ref[...]

        @pl.when(x + d >= ROW)
        def _(ref=ref):
            ref[0] = z2_ref[...]

        ref[1] = z1_ref[...]


def near_hidden(first, starts, block):
    rows = lax.broadcasted_iota(jnp.int32, (T, 1), 0)
    hidden = (rows + (first - block * ROW * T)) < starts
    if block == 0:
        hidden = hidden | (rows > lax.broadcasted_iota(jnp.int32, (1, T), 1))
    return hidden


def far_hidden(first, starts, behind):
    rows = lax.broadcasted_iota(jnp.int32, (T, 1), 0)
    return (rows + (first - behind * T)) < starts


def near_kernel(starts_ref, q_ref, g_ref, own_ref, z1_ref, z2_ref, m_ref, t_ref, r_ref):
    first = lax.axis_index("peer") * T
    starts = starts_ref[...]
    for i, ref in enumerate((own_ref, z1_ref, z2_ref)):
        scores(q_ref, g_ref, ref[0], ref[1], near_hidden(first, starts, i), i, m_ref, t_ref, r_ref)


def behind(d, kind, x):
    return jnp.where((x >= d) ^ (kind == 1), d, ROW + d)


def key_side(q_ref, g_ref, pb_ref, ds_ref):
    dk = sum(dot(ds_ref[h], head(q_ref, h), PLAIN) for h in range(H))
    dv = sum(dot(pb_ref[h], head(g_ref, h), PLAIN) for h in range(H))
    return dk * SCALE, dv


def far_scores(d, starts_ref, q_ref, g_ref, far_ref, p_ref, dp_ref, m_ref, t_ref, r_ref):
    peer = lax.axis_index("peer")
    first = peer * T
    starts = starts_ref[...]
    for i in range(2):
        hidden = far_hidden(first, starts, behind(d, i, lax.rem(peer, ROW)))
        scores(q_ref, g_ref, far_ref[i, 0], far_ref[i, 1], hidden, i, m_ref, t_ref, r_ref, p_ref, dp_ref)


def far_back(p_ref, dp_ref, w_ref, rd_ref, q_ref, g_ref, back_ref, pb_ref, ds_ref):
    for i in range(2):
        for h in range(H):
            pn = p_ref[i, h] * w_ref[i, h : h + 1]
            pb_ref[i, h] = pn.astype(BF16)
            ds_ref[i, h] = (pn * (dp_ref[i, h] - rd_ref[h : h + 1])).astype(BF16)
        dk, dv = key_side(q_ref, g_ref, pb_ref.at[i], ds_ref.at[i])
        back_ref[i, 0] = dk.astype(BF16)
        back_ref[i, 1] = dv.astype(BF16)


def last_kernel(
    starts_ref, q_ref, g_ref, far_ref, mn, tn, rn, m1, t1, r1, p2_ref, dp2_ref, m2, t2, r2,
    b2_ref, peak_ref, over_ref, rd_ref, w1_ref, w3_ref, p3_ref, dp3_ref,
    m_ref, t_ref, r_ref, w2_ref, pb_ref, ds_ref,
):
    far_scores(3, starts_ref, q_ref, g_ref, far_ref, p3_ref, dp3_ref, m_ref, t_ref, r_ref)

    def each(near, *pairs):
        return [near[b] for b in range(3)] + [ref[b] for ref in pairs for b in range(2)]

    peaks, totals, dots = each(mn, m1, m2, m_ref), each(tn, t1, t2, t_ref), each(rn, r1, r2, r_ref)
    peak = functools.reduce(jnp.maximum, peaks)
    factors = [jnp.exp2((m - peak) * TO_EXP2) for m in peaks]
    over = 1.0 / sum(f * t for f, t in zip(factors, totals))
    peak_ref[...] = peak
    over_ref[...] = over
    rd_ref[...] = sum(f * r for f, r in zip(factors, dots)) * over
    for n, ref in enumerate((w1_ref, w2_ref, w3_ref)):
        for b in range(2):
            ref[b] = factors[3 + 2 * n + b] * over
    far_back(p2_ref, dp2_ref, w2_ref, rd_ref, q_ref, g_ref, b2_ref, pb_ref, ds_ref)


def sides_kernel(q_ref, g_ref, rd_ref, p1_ref, dp1_ref, w1_ref, p3_ref, dp3_ref, w3_ref, b1_ref, b3_ref, pb_ref, ds_ref):
    far_back(p1_ref, dp1_ref, w1_ref, rd_ref, q_ref, g_ref, b1_ref, pb_ref, ds_ref)
    far_back(p3_ref, dp3_ref, w3_ref, rd_ref, q_ref, g_ref, b3_ref, pb_ref, ds_ref)


def weights(q_ref, g_ref, key, value, hidden, peak_ref, over_ref, rd_ref, pb_ref, ds_ref):
    for h in range(H):
        s = dot(key, head(q_ref, h), LONG)
        dp = dot(value, head(g_ref, h), LONG)
        s = jnp.where(hidden, NEG, s)
        pn = jnp.exp2((s - peak_ref[h : h + 1]) * TO_EXP2) * over_ref[h : h + 1]
        pb_ref[h] = pn.astype(BF16)
        ds_ref[h] = (pn * (dp - rd_ref[h : h + 1])).astype(BF16)


def query_side(key, value, pb_ref, ds_ref, o_ref, dq_ref, fresh):
    kt, vt = key.T, value.T
    for h in range(H):
        o, dq = dot(vt, pb_ref[h], PLAIN), dot(kt, ds_ref[h], PLAIN)
        o_ref[h] = o if fresh else o_ref[h] + o
        dq_ref[h] = dq if fresh else dq_ref[h] + dq


def near_back_kernel(
    starts_ref, q_ref, g_ref, own_ref, z1_ref, z2_ref, peak_ref, over_ref, rd_ref,
    near_ref, o_ref, dq_ref, pb_ref, ds_ref,
):
    first = lax.axis_index("peer") * T
    for b, ref in enumerate((own_ref, z1_ref, z2_ref)):
        pb, ds = pb_ref.at[b % 2], ds_ref.at[b % 2]
        hidden = near_hidden(first, starts_ref[...], b)
        weights(q_ref, g_ref, ref[0], ref[1], hidden, peak_ref, over_ref, rd_ref, pb, ds)
        near_ref[b, 0], near_ref[b, 1] = key_side(q_ref, g_ref, pb, ds)
        query_side(ref[0], ref[1], pb, ds, o_ref, dq_ref, b == 0)


def query_side_kernel(
    starts_ref, q_ref, g_ref, f1_ref, f2_ref, f3_ref, peak_ref, over_ref, rd_ref, o_ref, dq_in_ref, _,
    out_ref, dq_ref, o_acc, dq_acc, pb_ref, ds_ref,
):
    peer = lax.axis_index("peer")
    x = lax.rem(peer, ROW)
    first = peer * T
    for b in range(6):
        d, kind = b // 2 + 1, b % 2
        ref = (f1_ref, f2_ref, f3_ref)[d - 1]
        hidden = far_hidden(first, starts_ref[...], behind(d, kind, x))
        pb, ds = pb_ref.at[b % 2], ds_ref.at[b % 2]
        weights(q_ref, g_ref, ref[kind, 0], ref[kind, 1], hidden, peak_ref, over_ref, rd_ref, pb, ds)
        query_side(ref[kind, 0], ref[kind, 1], pb, ds, o_acc, dq_acc, b == 0)

    for h in range(H):
        out_ref[:, h * D : (h + 1) * D] = (o_acc[h] + o_ref[h]).T.astype(BF16)
        dq_ref[:, h * D : (h + 1) * D] = (dq_acc[h] + dq_in_ref[h]).T * SCALE


def add_back(d, ref, own, one, two):
    same = lax.rem(lax.axis_index("peer"), ROW) + d < ROW
    a, b = ref[0].astype(F32), ref[1].astype(F32)
    return own + jnp.where(same, a, 0.0), one + b, two + jnp.where(same, 0.0, a)


def gather_first_kernel(mine_ref, r2_ref, out_ref):
    for i, total in enumerate(add_back(2, r2_ref, mine_ref[0], mine_ref[1], mine_ref[2])):
        out_ref[i] = total


def gather_one_kernel(mine_ref, r1_ref, out_ref):
    for i, total in enumerate(add_back(1, r1_ref, mine_ref[0], mine_ref[1], mine_ref[2])):
        out_ref[i] = total


def gather_kernel(mine_ref, r3_ref, own_ref, one_ref, two_ref):
    own, one, two = add_back(3, r3_ref, mine_ref[0], mine_ref[1], mine_ref[2])
    own_ref[...] = own
    one_ref[...] = one.astype(BF16)
    two_ref[...] = two.astype(BF16)


def add_two_kernel(own_ref, two_ref, out_ref):
    out_ref[...] = own_ref[...] + two_ref[...].astype(F32)


def final_kernel(own_ref, one_ref, dk_ref, dv_ref):
    dk_ref[...] = own_ref[0] + one_ref[0].astype(F32)
    dv_ref[...] = own_ref[1] + one_ref[1].astype(F32)


def along_z(block, rows, peers):
    far = rows * ROW
    return lax.ppermute(block, "peer", [(i, i + far) for i in range(peers) if 0 <= i + far < peers])


def along_x(block, columns, peers):
    return lax.ppermute(block, "peer", [(i, i - i % ROW + (i + columns) % ROW) for i in range(peers)])


def call(kernel, out, specs, scratch=(), blocks=0, limit=24, first=VM):
    return pl.pallas_call(
        kernel,
        out_shape=out,
        in_specs=specs,
        out_specs=(first,) + tuple(VM for _ in out[1:]),
        scratch_shapes=list(scratch),
        compiler_params=pltpu.CompilerParams(vmem_limit_bytes=limit << 20),
        cost_estimate=pl.CostEstimate(
            flops=blocks * H * T * T * D * 4, bytes_accessed=1 << 20, transcendentals=blocks * H * T * T
        ),
    )


def body(queries, keys, values, grad_out, doc_lengths):
    peers = lax.axis_size("peer")
    array = jax.ShapeDtypeStruct
    block, stats = (2, T, D), (H, T)
    pair = array((2, *block), BF16)
    tiles, sums = (array((2, H, T, T), F32),) * 2, (array((2, *stats), F32),) * 3
    staged = [pltpu.VMEM((2, H, T, T), BF16)] * 2
    (own,) = call(pair_kernel, (pltpu.VMEM(block, BF16),), [ANY] * 2, [pltpu.SemaphoreType.DMA((2,))], limit=54)(
        keys, values
    )
    z1 = along_z(own, 1, peers)
    z2 = along_z(own, 2, peers)
    queries, grad_out, starts = call(
        hold_kernel,
        (array((T, H * D), BF16), array((T, H * D), BF16), array((1, T), jnp.int32)),
        [SM] + [VM] * 2,
        blocks=1,
        limit=4,
    )(doc_lengths, queries, grad_out)
    wanted = (starts, queries, grad_out)
    packed = call(pack_kernel, (pair,) * 3, [VM] * 4, limit=4)(starts, own, z1, z2)
    f1, f2, f3 = (along_x(p, d, peers) for d, p in enumerate(packed, 1))
    near = call(near_kernel, (array((3, *stats), F32),) * 3, [VM] * 6, blocks=3, limit=8)(*wanted, own, z1, z2)
    arrive = {d: call(functools.partial(far_scores, d), tiles + sums, [VM] * 4, blocks=2, limit=8) for d in (1, 2)}
    p2, dp2, *sums2 = arrive[2](*wanted, f2)
    p1, dp1, *sums1 = arrive[1](*wanted, f1)
    b2, peak, over, rd, w1, w3, p3, dp3 = call(
        last_kernel,
        (pair,) + (array(stats, F32),) * 3 + (array((2, *stats), F32),) * 2 + tiles,
        [VM] * 15,
        [pltpu.VMEM((2, *stats), F32)] * 4 + staged,
        blocks=4,
        limit=8,
    )(*wanted, f3, *near, *sums1, p2, dp2, *sums2)
    r2 = along_x(b2, -2, peers)
    b1, b3 = call(sides_kernel, (pair,) * 2, [VM] * 9, staged, blocks=4, limit=8)(
        queries, grad_out, rd, p1, dp1, w1, p3, dp3, w3
    )
    r1, r3 = along_x(b1, -1, peers), along_x(b3, -3, peers)
    mine, near_o, near_dq = call(
        near_back_kernel,
        (array((3, *block), F32),) + (array((H, D, T), F32),) * 2,
        [VM] * 9,
        staged,
        blocks=3,
        limit=8,
    )(*wanted, own, z1, z2, peak, over, rd)
    (mine,) = call(gather_first_kernel, (array((3, *block), F32),), [VM] * 2, limit=4)(mine, r2)
    (mine,) = call(gather_one_kernel, (array((3, *block), F32),), [VM] * 2, limit=4)(mine, r1)
    mine, one, two = call(
        gather_kernel, (array(block, F32), array(block, BF16), array(block, BF16)), [VM] * 2, limit=4
    )(mine, r3)
    attended, query_grad = call(
        query_side_kernel,
        (array((T, H * D), BF16), array((T, H * D), F32)),
        [VM] * 12,
        [pltpu.VMEM((H, D, T), F32)] * 2 + staged,
        blocks=9,
        limit=16,
    )(*wanted, f1, f2, f3, peak, over, rd, near_o, near_dq, one)
    two, one = along_z(two, -2, peers), along_z(one, -1, peers)
    (mine,) = call(add_two_kernel, (array(block, F32),), [VM] * 2, limit=4)(mine, two)
    key_grad, value_grad = call(final_kernel, (array((T, D), F32),) * 2, [VM] * 2, limit=4)(mine, one)
    return attended, query_grad, key_grad, value_grad


def solution(mesh):
    tokens = P("peer", "head")
    return jax.shard_map(
        body,
        mesh=mesh,
        in_specs=(tokens, tokens, tokens, tokens, P()),
        out_specs=(tokens, tokens, tokens, tokens),
        check_vma=False,
    )
```

```python
import functools
import math

import jax
import jax.numpy as jnp
from jax import lax
from jax.experimental import pallas as pl
from jax.experimental.pallas import tpu as pltpu
from jax.sharding import PartitionSpec as P

T = 256
D = 128
H = 4
ROW = 4
F32 = jnp.float32
BF16 = jnp.bfloat16
NEG = -1e30
SCALE = D**-0.5
TO_EXP2 = SCALE * math.log2(math.e)
LONG = (((1,), (1,)), ((), ()))
PLAIN = (((1,), (0,)), ((), ()))
VM = pl.BlockSpec(memory_space=pltpu.VMEM)
ANY = pl.BlockSpec(memory_space=pl.ANY)
SM = pl.BlockSpec(memory_space=pltpu.SMEM)


def dot(a, b, dims):
    return lax.dot_general(a, b, dims, preferred_element_type=F32)


def head(ref, h):
    return ref[:, h * D : (h + 1) * D]


def doc_starts(lengths_ref, first):
    place = first + lax.broadcasted_iota(jnp.int32, (1, T), 1)
    start = jnp.int32(0)
    own = jnp.zeros((1, T), jnp.int32)
    for i in range(lengths_ref.shape[0]):
        own = jnp.where(place >= start, start, own)
        start = start + lengths_ref[i]
    return own


def scores(q_ref, g_ref, key, value, hidden, index, m_ref, t_ref, r_ref, p_ref=None, dp_ref=None):
    for h in range(H):
        s = dot(key, head(q_ref, h), LONG)
        dp = dot(value, head(g_ref, h), LONG)
        s = jnp.where(hidden, NEG, s)
        m = jnp.max(s, axis=0, keepdims=True)
        p = jnp.exp2((s - m) * TO_EXP2)
        if p_ref is not None:
            p_ref[index, h] = p
            dp_ref[index, h] = dp
        m_ref[index, h : h + 1] = m
        t_ref[index, h : h + 1] = jnp.sum(p, axis=0, keepdims=True)
        r_ref[index, h : h + 1] = jnp.sum(p * dp, axis=0, keepdims=True)


def pair_kernel(k_ref, v_ref, out_ref, sem):
    copies = [pltpu.make_async_copy(r, out_ref.at[i], sem.at[i]) for i, r in enumerate((k_ref, v_ref))]
    for copy in copies:
        copy.start()
    for copy in copies:
        copy.wait()


def hold_kernel(lengths_ref, q_ref, g_ref, q_out, g_out, starts_ref):
    q_out[...] = q_ref[...]
    g_out[...] = g_ref[...]
    starts_ref[...] = doc_starts(lengths_ref, lax.axis_index("peer") * T)


def pack_kernel(_, own_ref, z1_ref, z2_ref, *out_refs):
    x = lax.rem(lax.axis_index("peer"), ROW)
    for d, ref in enumerate(out_refs, 1):

        @pl.when(x + d < ROW)
        def _(ref=ref):
            ref[0] = own_ref[...]

        @pl.when(x + d >= ROW)
        def _(ref=ref):
            ref[0] = z2_ref[...]

        ref[1] = z1_ref[...]


def near_hidden(first, starts, block):
    rows = lax.broadcasted_iota(jnp.int32, (T, 1), 0)
    hidden = (rows + (first - block * ROW * T)) < starts
    if block == 0:
        hidden = hidden | (rows > lax.broadcasted_iota(jnp.int32, (1, T), 1))
    return hidden


def far_hidden(first, starts, behind):
    rows = lax.broadcasted_iota(jnp.int32, (T, 1), 0)
    return (rows + (first - behind * T)) < starts


def near_kernel(starts_ref, q_ref, g_ref, own_ref, z1_ref, z2_ref, m_ref, t_ref, r_ref):
    first = lax.axis_index("peer") * T
    starts = starts_ref[...]
    for i, ref in enumerate((own_ref, z1_ref, z2_ref)):
        scores(q_ref, g_ref, ref[0], ref[1], near_hidden(first, starts, i), i, m_ref, t_ref, r_ref)


def behind(d, kind, x):
    return jnp.where((x >= d) ^ (kind == 1), d, ROW + d)


def key_side(q_ref, g_ref, pb_ref, ds_ref):
    dk = sum(dot(ds_ref[h], head(q_ref, h), PLAIN) for h in range(H))
    dv = sum(dot(pb_ref[h], head(g_ref, h), PLAIN) for h in range(H))
    return dk * SCALE, dv


def far_scores(d, starts_ref, q_ref, g_ref, far_ref, p_ref, dp_ref, m_ref, t_ref, r_ref):
    peer = lax.axis_index("peer")
    first = peer * T
    starts = starts_ref[...]
    for i in range(2):
        hidden = far_hidden(first, starts, behind(d, i, lax.rem(peer, ROW)))
        scores(q_ref, g_ref, far_ref[i, 0], far_ref[i, 1], hidden, i, m_ref, t_ref, r_ref, p_ref, dp_ref)


def far_back(p_ref, dp_ref, w_ref, rd_ref, q_ref, g_ref, back_ref, pb_ref, ds_ref):
    for i in range(2):
        for h in range(H):
            pn = p_ref[i, h] * w_ref[i, h : h + 1]
            pb_ref[i, h] = pn.astype(BF16)
            ds_ref[i, h] = (pn * (dp_ref[i, h] - rd_ref[h : h + 1])).astype(BF16)
        dk, dv = key_side(q_ref, g_ref, pb_ref.at[i], ds_ref.at[i])
        back_ref[i, 0] = dk.astype(BF16)
        back_ref[i, 1] = dv.astype(BF16)


def last_kernel(
    starts_ref, q_ref, g_ref, far_ref, mn, tn, rn, m1, t1, r1, p2_ref, dp2_ref, m2, t2, r2,
    b2_ref, peak_ref, over_ref, rd_ref, w1_ref, w3_ref, p3_ref, dp3_ref,
    m_ref, t_ref, r_ref, w2_ref, pb_ref, ds_ref,
):
    far_scores(3, starts_ref, q_ref, g_ref, far_ref, p3_ref, dp3_ref, m_ref, t_ref, r_ref)

    def each(near, *pairs):
        return [near[b] for b in range(3)] + [ref[b] for ref in pairs for b in range(2)]

    peaks, totals, dots = each(mn, m1, m2, m_ref), each(tn, t1, t2, t_ref), each(rn, r1, r2, r_ref)
    peak = functools.reduce(jnp.maximum, peaks)
    factors = [jnp.exp2((m - peak) * TO_EXP2) for m in peaks]
    over = 1.0 / sum(f * t for f, t in zip(factors, totals))
    peak_ref[...] = peak
    over_ref[...] = over
    rd_ref[...] = sum(f * r for f, r in zip(factors, dots)) * over
    for n, ref in enumerate((w1_ref, w2_ref, w3_ref)):
        for b in range(2):
            ref[b] = factors[3 + 2 * n + b] * over
    far_back(p2_ref, dp2_ref, w2_ref, rd_ref, q_ref, g_ref, b2_ref, pb_ref, ds_ref)


def sides_kernel(q_ref, g_ref, rd_ref, p1_ref, dp1_ref, w1_ref, p3_ref, dp3_ref, w3_ref, b1_ref, b3_ref, pb_ref, ds_ref):
    far_back(p1_ref, dp1_ref, w1_ref, rd_ref, q_ref, g_ref, b1_ref, pb_ref, ds_ref)
    far_back(p3_ref, dp3_ref, w3_ref, rd_ref, q_ref, g_ref, b3_ref, pb_ref, ds_ref)


def weights(q_ref, g_ref, key, value, hidden, peak_ref, over_ref, rd_ref, pb_ref, ds_ref):
    for h in range(H):
        s = dot(key, head(q_ref, h), LONG)
        dp = dot(value, head(g_ref, h), LONG)
        s = jnp.where(hidden, NEG, s)
        pn = jnp.exp2((s - peak_ref[h : h + 1]) * TO_EXP2) * over_ref[h : h + 1]
        pb_ref[h] = pn.astype(BF16)
        ds_ref[h] = (pn * (dp - rd_ref[h : h + 1])).astype(BF16)


def query_side(key, value, pb_ref, ds_ref, o_ref, dq_ref, fresh):
    kt, vt = key.T, value.T
    for h in range(H):
        o, dq = dot(vt, pb_ref[h], PLAIN), dot(kt, ds_ref[h], PLAIN)
        o_ref[h] = o if fresh else o_ref[h] + o
        dq_ref[h] = dq if fresh else dq_ref[h] + dq


def near_back_kernel(
    starts_ref, q_ref, g_ref, own_ref, z1_ref, z2_ref, peak_ref, over_ref, rd_ref,
    near_ref, o_ref, dq_ref, pb_ref, ds_ref,
):
    first = lax.axis_index("peer") * T
    for b, ref in enumerate((own_ref, z1_ref, z2_ref)):
        pb, ds = pb_ref.at[b % 2], ds_ref.at[b % 2]
        hidden = near_hidden(first, starts_ref[...], b)
        weights(q_ref, g_ref, ref[0], ref[1], hidden, peak_ref, over_ref, rd_ref, pb, ds)
        near_ref[b, 0], near_ref[b, 1] = key_side(q_ref, g_ref, pb, ds)
        query_side(ref[0], ref[1], pb, ds, o_ref, dq_ref, b == 0)


def query_side_kernel(
    starts_ref, q_ref, g_ref, f1_ref, f2_ref, f3_ref, peak_ref, over_ref, rd_ref, o_ref, dq_in_ref, _,
    out_ref, dq_ref, o_acc, dq_acc, pb_ref, ds_ref,
):
    peer = lax.axis_index("peer")
    x = lax.rem(peer, ROW)
    first = peer * T
    for b in range(6):
        d, kind = b // 2 + 1, b % 2
        ref = (f1_ref, f2_ref, f3_ref)[d - 1]
        hidden = far_hidden(first, starts_ref[...], behind(d, kind, x))
        pb, ds = pb_ref.at[b % 2], ds_ref.at[b % 2]
        weights(q_ref, g_ref, ref[kind, 0], ref[kind, 1], hidden, peak_ref, over_ref, rd_ref, pb, ds)
        query_side(ref[kind, 0], ref[kind, 1], pb, ds, o_acc, dq_acc, b == 0)

    for h in range(H):
        out_ref[:, h * D : (h + 1) * D] = (o_acc[h] + o_ref[h]).T.astype(BF16)
        dq_ref[:, h * D : (h + 1) * D] = (dq_acc[h] + dq_in_ref[h]).T * SCALE


def add_back(d, ref, own, one, two):
    same = lax.rem(lax.axis_index("peer"), ROW) + d < ROW
    a, b = ref[0].astype(F32), ref[1].astype(F32)
    return own + jnp.where(same, a, 0.0), one + b, two + jnp.where(same, 0.0, a)


def gather_first_kernel(mine_ref, r2_ref, out_ref):
    for i, total in enumerate(add_back(2, r2_ref, mine_ref[0], mine_ref[1], mine_ref[2])):
        out_ref[i] = total


def gather_one_kernel(mine_ref, r1_ref, out_ref):
    for i, total in enumerate(add_back(1, r1_ref, mine_ref[0], mine_ref[1], mine_ref[2])):
        out_ref[i] = total


def gather_kernel(mine_ref, r3_ref, own_ref, one_ref, two_ref):
    own, one, two = add_back(3, r3_ref, mine_ref[0], mine_ref[1], mine_ref[2])
    own_ref[...] = own
    one_ref[...] = one.astype(BF16)
    two_ref[...] = two.astype(BF16)


def add_kernel(own_ref, one_ref, out_ref):
    out_ref[...] = own_ref[...] + one_ref[...].astype(F32)


def final_kernel(own_ref, two_ref, dk_ref, dv_ref):
    dk_ref[...] = own_ref[0] + two_ref[0].astype(F32)
    dv_ref[...] = own_ref[1] + two_ref[1].astype(F32)


def along_z(block, rows, peers):
    far = rows * ROW
    return lax.ppermute(block, "peer", [(i, i + far) for i in range(peers) if 0 <= i + far < peers])


def along_x(block, columns, peers):
    return lax.ppermute(block, "peer", [(i, i - i % ROW + (i + columns) % ROW) for i in range(peers)])


def call(kernel, out, specs, scratch=(), blocks=0, limit=24, first=VM):
    return pl.pallas_call(
        kernel,
        out_shape=out,
        in_specs=specs,
        out_specs=(first,) + tuple(VM for _ in out[1:]),
        scratch_shapes=list(scratch),
        compiler_params=pltpu.CompilerParams(vmem_limit_bytes=limit << 20),
        cost_estimate=pl.CostEstimate(
            flops=blocks * H * T * T * D * 4, bytes_accessed=1 << 20, transcendentals=blocks * H * T * T
        ),
    )


def body(queries, keys, values, grad_out, doc_lengths):
    peers = lax.axis_size("peer")
    array = jax.ShapeDtypeStruct
    block, stats = (2, T, D), (H, T)
    pair = array((2, *block), BF16)
    tiles, sums = (array((2, H, T, T), F32),) * 2, (array((2, *stats), F32),) * 3
    staged = [pltpu.VMEM((2, H, T, T), BF16)] * 2
    (own,) = call(pair_kernel, (pltpu.VMEM(block, BF16),), [ANY] * 2, [pltpu.SemaphoreType.DMA((2,))], limit=54)(
        keys, values
    )
    z1 = along_z(own, 1, peers)
    z2 = along_z(own, 2, peers)
    queries, grad_out, starts = call(
        hold_kernel,
        (array((T, H * D), BF16), array((T, H * D), BF16), array((1, T), jnp.int32)),
        [SM] + [VM] * 2,
        blocks=1,
        limit=4,
    )(doc_lengths, queries, grad_out)
    wanted = (starts, queries, grad_out)
    packed = call(pack_kernel, (pair,) * 3, [VM] * 4, limit=4)(starts, own, z1, z2)
    f1, f2, f3 = (along_x(p, d, peers) for d, p in enumerate(packed, 1))
    near = call(near_kernel, (array((3, *stats), F32),) * 3, [VM] * 6, blocks=3, limit=8)(*wanted, own, z1, z2)
    arrive = {d: call(functools.partial(far_scores, d), tiles + sums, [VM] * 4, blocks=2, limit=8) for d in (1, 2)}
    p2, dp2, *sums2 = arrive[2](*wanted, f2)
    p1, dp1, *sums1 = arrive[1](*wanted, f1)
    b2, peak, over, rd, w1, w3, p3, dp3 = call(
        last_kernel,
        (pair,) + (array(stats, F32),) * 3 + (array((2, *stats), F32),) * 2 + tiles,
        [VM] * 15,
        [pltpu.VMEM((2, *stats), F32)] * 4 + staged,
        blocks=4,
        limit=8,
    )(*wanted, f3, *near, *sums1, p2, dp2, *sums2)
    r2 = along_x(b2, -2, peers)
    b1, b3 = call(sides_kernel, (pair,) * 2, [VM] * 9, staged, blocks=4, limit=8)(
        queries, grad_out, rd, p1, dp1, w1, p3, dp3, w3
    )
    r1, r3 = along_x(b1, -1, peers), along_x(b3, -3, peers)
    mine, near_o, near_dq = call(
        near_back_kernel,
        (array((3, *block), F32),) + (array((H, D, T), F32),) * 2,
        [VM] * 9,
        staged,
        blocks=3,
        limit=8,
    )(*wanted, own, z1, z2, peak, over, rd)
    (mine,) = call(gather_first_kernel, (array((3, *block), F32),), [VM] * 2, limit=4)(mine, r2)
    (mine,) = call(gather_one_kernel, (array((3, *block), F32),), [VM] * 2, limit=4)(mine, r1)
    mine, one, two = call(
        gather_kernel, (array(block, F32), array(block, BF16), array(block, BF16)), [VM] * 2, limit=4
    )(mine, r3)
    attended, query_grad = call(
        query_side_kernel,
        (array((T, H * D), BF16), array((T, H * D), F32)),
        [VM] * 12,
        [pltpu.VMEM((H, D, T), F32)] * 2 + staged,
        blocks=9,
        limit=16,
    )(*wanted, f1, f2, f3, peak, over, rd, near_o, near_dq, one)
    two, one = along_z(two, -2, peers), along_z(one, -1, peers)
    (mine,) = call(add_kernel, (array(block, F32),), [VM] * 2, limit=4)(mine, one)
    key_grad, value_grad = call(final_kernel, (array((T, D), F32),) * 2, [VM] * 2, limit=4)(mine, two)
    return attended, query_grad, key_grad, value_grad


def solution(mesh):
    tokens = P("peer", "head")
    return jax.shard_map(
        body,
        mesh=mesh,
        in_specs=(tokens, tokens, tokens, tokens, P()),
        out_specs=(tokens, tokens, tokens, tokens),
        check_vma=False,
    )
```
